256 devices in a mesh: dom: 256 (over x, z, y, core).
Axes of the slice: x: 4, y: 4, z: 8, core: 2. Of those that a mesh axis runs over, the one named last changes fastest.
Arguments:
- dof_state: float32 [9, 56, 229376], P(None, None, 'dom'), may hold values from -6 to 6
- jacobian_inv: float32 [3, 3, 229376], P(None, None, 'dom'), may hold values from -3.5 to 3.5
- face_normals: float32 [4, 3, 229376], P(None, None, 'dom'), may hold values from -3 to 3
- material: float32 [3, 229376], P(None, 'dom'), may hold values from 0.3 to 4.5, as said below
- deriv_mats: float32 [3, 35, 56], replicated, may hold values from -0.75 to 0.75
- stiff_mats: float32 [3, 56, 56], replicated, may hold values from -0.75 to 0.75
- trace_mats: float32 [4, 21, 56], replicated, may hold values from -0.75 to 0.75
- lift_mats: float32 [4, 56, 21], replicated, may hold values from -1.25 to 1.25
- orient_mats: float32 [3, 21, 21], replicated, may hold values from -1.25 to 1.25
- nbr_slot: int32 [4, 229376], P(None, 'dom'), may hold values from 0 to 1279, as said below
- nbr_face: int32 [4, 229376], P(None, 'dom'), may hold values from 0 to 3, as said below
- orient_code: int32 [4, 229376], P(None, 'dom'), may hold values from 0 to 2
- send_list: int32 [4, 3, 8192], P(None, None, 'dom'), may hold values from -1 to 3583, as said below
Outputs:
- new_state: float32 [9, 56, 229376], P(None, None, 'dom')
The draws below stay inside these ranges and needn't reach their ends.
Inputs may be any that keep to these rules, and one draw needn't show every extreme that they name: `send_list`: entry [p, c, d * 32 + k] is what device d sends as slot k of its list for peer p (device d + offset_p with offsets -2, -1, +1, +2, wrapping) and receiving cluster c: sender element * 4 + face, live entries first, then -1. `nbr_slot`: below 896: a local element. Else 896 + (p * 3 + c) * 32 + k: live slot k of the list that device (own - offset_p) sends for peer p and cluster c, where c is this element's cluster; every live slot is named by exactly one face. `nbr_face`: for a face that names a slot, the face stored in that slot's entry. `material`: rows are density, first Lame parameter, shear modulus.
All inputs are finite; a program needn't handle non-finite values.
Results may differ from the reference program's by a relative error of at most 0.0003.
Values sent between devices are 32-bit elements; how exact they have to be, the bound alone decides.
A program may use at most 192 MiB of HBM per device.

```python
import math
import jax
import jax.numpy as jnp
from jax import lax

NB = 56
NQ = 9
NF = 21
BLK = 128
CAPC = 32
PEERS = 4
ELEMS = 896
MESH_ELEMS = 229376
N_DOM = 256


peer_shifts = (-2, -1, 1, 2)


def face_links(key):
    count_key, entry_key, face_key, perm_key, local_key, lface_key = jax.random.split(key, 6)
    live_counts = jax.random.randint(count_key, (N_DOM, PEERS, 3), CAPC // 4, CAPC + 1)
    dev_grid = jnp.arange(N_DOM)[:, None, None]
    peer_grid = jnp.arange(PEERS)[None, :, None]
    clus_grid = jnp.arange(3)[None, None, :]
    first_dev = dev_grid == 0
    live_counts = jnp.where(first_dev & (peer_grid == 0) & (clus_grid == 0), CAPC, live_counts)
    live_counts = jnp.where(first_dev & (peer_grid == PEERS - 1) & (clus_grid == 2), CAPC, live_counts)
    live_counts = jnp.where(first_dev & (peer_grid == 1) & (clus_grid == 0), CAPC // 4, live_counts)
    elems_sent = jax.random.randint(entry_key, (N_DOM, PEERS, 3, CAPC), 0, ELEMS)
    faces_sent = jax.random.randint(face_key, (N_DOM, PEERS, 3, CAPC), 0, 4)
    elems_sent = elems_sent.at[0, 0, 0, 0].set(ELEMS - 1)
    faces_sent = faces_sent.at[0, 0, 0, 0].set(3)
    is_live = jnp.arange(CAPC)[None, None, None, :] < live_counts[..., None]
    entry_grid = jnp.where(is_live, elems_sent * 4 + faces_sent, -1).astype(jnp.int32)
    send_table = jnp.transpose(entry_grid, (1, 2, 0, 3)).reshape(PEERS, 3, N_DOM * CAPC)
    offset_table = jnp.array(peer_shifts, jnp.int32)
    sender_of = (jnp.arange(N_DOM, dtype=jnp.int32)[:, None] - offset_table[None, :]) % N_DOM
    peer_index = jnp.arange(PEERS)[None, :]
    recv_counts = live_counts[sender_of, peer_index]
    recv_entries = entry_grid[sender_of, peer_index]
    slot_parts = []
    face_parts = []
    for cluster in range(3):
        blk_size = BLK * 2 ** cluster
        pool_size = 4 * blk_size
        row_keys = jax.random.split(jax.random.fold_in(perm_key, cluster), N_DOM)
        shuffled = jax.vmap(lambda one_key: jax.random.permutation(one_key, pool_size))(row_keys)
        clus_counts = recv_counts[:, :, cluster]
        run_ends = jnp.cumsum(clus_counts, axis=1)
        run_begins = run_ends - clus_counts
        positions = jnp.arange(pool_size)[None, :]
        peer_of = jnp.sum((positions[:, :, None] >= run_ends[:, None, :]).astype(jnp.int32), axis=2)
        is_remote = peer_of < PEERS
        peer_of = jnp.minimum(peer_of, PEERS - 1)
        begin_of = jnp.take_along_axis(run_begins, peer_of, axis=1)
        slot_of = jnp.clip(positions - begin_of, 0, CAPC - 1)
        flat_entries = recv_entries[:, :, cluster, :].reshape(N_DOM, PEERS * CAPC)
        entry_of = jnp.take_along_axis(flat_entries, peer_of * CAPC + slot_of, axis=1)
        ghost_slot = ELEMS + (peer_of * 3 + cluster) * CAPC + slot_of
        local_elem = jax.random.randint(jax.random.fold_in(local_key, cluster), (N_DOM, pool_size), 0, ELEMS)
        local_face = jax.random.randint(jax.random.fold_in(lface_key, cluster), (N_DOM, pool_size), 0, 4)
        slot_value = jnp.where(is_remote, ghost_slot, local_elem).astype(jnp.int32)
        face_value = jnp.where(is_remote, entry_of % 4, local_face).astype(jnp.int32)
        face_pos = shuffled // blk_size
        elem_pos = shuffled % blk_size
        row_index = jnp.broadcast_to(jnp.arange(N_DOM)[:, None], (N_DOM, pool_size))
        slot_grid = jnp.zeros((N_DOM, 4, blk_size), jnp.int32).at[row_index, face_pos, elem_pos].set(slot_value)
        face_grid = jnp.zeros((N_DOM, 4, blk_size), jnp.int32).at[row_index, face_pos, elem_pos].set(face_value)
        slot_parts.append(slot_grid)
        face_parts.append(face_grid)
    slot_all = jnp.transpose(jnp.concatenate(slot_parts, axis=2), (1, 0, 2)).reshape(4, MESH_ELEMS)
    face_all = jnp.transpose(jnp.concatenate(face_parts, axis=2), (1, 0, 2)).reshape(4, MESH_ELEMS)
    return (slot_all, face_all, send_table)


def draw_nbr_slot(key, part):
    return face_links(key)[0]


def draw_nbr_face(key, part):
    return face_links(key)[1]


def draw_send_list(key, part):
    return face_links(key)[2]


def draw_material(key, part):
    key = jax.random.fold_in(key, 11)
    first_key, second_key, third_key = jax.random.split(key, 3)
    position = jnp.arange(MESH_ELEMS, dtype=jnp.float32) / (MESH_ELEMS - 1)
    stiffen = 1.0 + 2.0 * position
    density = jnp.exp(jax.random.uniform(first_key, (MESH_ELEMS,), jnp.float32, 0.0, 0.9))
    lame_first = jnp.exp(jax.random.uniform(second_key, (MESH_ELEMS,), jnp.float32, -0.69, 0.4)) * stiffen
    shear_mod = jnp.exp(jax.random.uniform(third_key, (MESH_ELEMS,), jnp.float32, -1.2, 0.0)) * stiffen
    return jnp.stack([density, lame_first, shear_mod])


def place_ends(drawn, own_key, low, high):
    dims = drawn.shape
    spot = [jax.random.randint(jax.random.fold_in(own_key, axis), (), 0, dims[axis]) for axis in range(len(dims))]
    drawn = drawn.at[tuple(spot)].set(low)
    longest = dims.index(max(dims))
    spot[longest] = (spot[longest] + 1) % dims[longest]
    return drawn.at[tuple(spot)].set(high)


def block_levels(stream_key, dims, cuts, least, top_value):
    gain = 1.0
    for dim, shards_of in cuts:
        draws = jax.random.uniform(jax.random.fold_in(jax.random.fold_in(stream_key, 6), dim), (shards_of,), jnp.float32, least / len(cuts), top_value / len(cuts))
        gain = gain * jnp.repeat(jnp.exp(draws), dims[dim] // shards_of).reshape((-1,) + (1,) * (len(dims) - 1 - dim))
    return gain


def centred(key, dims, scale, bound, shards=(), kind=jnp.bfloat16):
    factor_of = block_levels(key, dims, shards, -0.22, 0.18) if shards else 1.0
    result = jax.random.normal(key, dims, jnp.float32) * scale * factor_of
    return jnp.minimum(jnp.maximum(result, -bound), bound).astype(kind)


def setup_inputs(seed: int = 0) -> dict:
    key_of = jax.random.split(jax.random.key(seed), 14)
    dof_state = centred(key_of[0], (NQ, NB, MESH_ELEMS), 1.0, 6.0, ((2, 256),), jnp.float32)
    jacobian_inv = centred(key_of[1], (3, 3, MESH_ELEMS), 3 ** -0.5, 3.5, ((2, 256),), jnp.float32)
    face_normals = centred(key_of[2], (4, 3, MESH_ELEMS), 0.5, 3.0, ((2, 256),), jnp.float32)
    material = draw_material(jax.random.fold_in(key_of[13], 71), 0)
    deriv_mats = centred(key_of[4], (3, 35, NB), NB ** -0.5, 0.75, (), jnp.float32)
    stiff_mats = centred(key_of[5], (3, NB, NB), NB ** -0.5, 0.75, (), jnp.float32)
    trace_mats = centred(key_of[6], (4, NF, NB), NB ** -0.5, 0.75, (), jnp.float32)
    lift_mats = centred(key_of[7], (4, NB, NF), NF ** -0.5, 1.25, (), jnp.float32)
    orient_mats = centred(key_of[8], (3, NF, NF), NF ** -0.5, 1.25, (), jnp.float32)
    nbr_slot = draw_nbr_slot(jax.random.fold_in(key_of[13], 71), 0)
    nbr_face = draw_nbr_face(jax.random.fold_in(key_of[13], 71), 0)
    orient_code = place_ends(jax.random.randint(key_of[11], (4, MESH_ELEMS), 0, 3), jax.random.fold_in(key_of[11], 1), 0, 2).astype(jnp.int32)
    send_list = draw_send_list(jax.random.fold_in(key_of[13], 71), 0)
    return dict(dof_state=dof_state, jacobian_inv=jacobian_inv, face_normals=face_normals, material=material, deriv_mats=deriv_mats, stiff_mats=stiff_mats, trace_mats=trace_mats, lift_mats=lift_mats, orient_mats=orient_mats, nbr_slot=nbr_slot, nbr_face=nbr_face, orient_code=orient_code, send_list=send_list)


step_size = 0.04
peer_offsets = (-2, -1, 1, 2)
level_dims = (56, 35, 20, 10, 4, 1)
highest = lax.Precision.HIGHEST

def star_apply(along, values_in, lame_first, shear_mod, inv_density):
    along_x, along_y, along_z = along
    stress_xx, stress_yy, stress_zz = (values_in[0], values_in[1], values_in[2])
    stress_xy, stress_yz, stress_xz = (values_in[3], values_in[4], values_in[5])
    speed_u, speed_v, speed_w = (values_in[6], values_in[7], values_in[8])
    longit = lame_first + 2.0 * shear_mod
    row_list = [-(longit * along_x * speed_u + lame_first * along_y * speed_v + lame_first * along_z * speed_w), -(lame_first * along_x * speed_u + longit * along_y * speed_v + lame_first * along_z * speed_w), -(lame_first * along_x * speed_u + lame_first * along_y * speed_v + longit * along_z * speed_w), -shear_mod * (along_y * speed_u + along_x * speed_v), -shear_mod * (along_z * speed_v + along_y * speed_w), -shear_mod * (along_z * speed_u + along_x * speed_w), -inv_density * (along_x * stress_xx + along_y * stress_xy + along_z * stress_xz), -inv_density * (along_x * stress_xy + along_y * stress_yy + along_z * stress_yz), -inv_density * (along_x * stress_xz + along_y * stress_yz + along_z * stress_zz)]
    return jnp.stack(row_list)

def taylor_levels(block, deriv_mats, jac_rows, lame_first, shear_mod, inv_density):
    levels = [block]
    current = block
    for level_num in range(5):
        rows_out = level_dims[level_num + 1]
        rows_in = level_dims[level_num]
        stacked = deriv_mats[:, :rows_out, :rows_in].reshape(3 * rows_out, rows_in)
        derived_vals = jnp.einsum('ab,qbe->qae', stacked, current, precision=highest)
        total_sum = None
        for ref_dir in range(3):
            contrib = star_apply(jac_rows[ref_dir], derived_vals[:, ref_dir * rows_out:(ref_dir + 1) * rows_out, :], lame_first, shear_mod, inv_density)
            total_sum = contrib if total_sum is None else total_sum + contrib
        current = -total_sum
        levels.append(current)
    return levels

def time_weights(lower, upper):
    return [step_size ** (level_num + 1) * (upper ** (level_num + 1) - lower ** (level_num + 1)) / math.factorial(level_num + 1) for level_num in range(6)]

def integrate(levels, weights):
    total_sum = levels[0] * weights[0]
    for level_num in range(1, 6):
        padding = 56 - levels[level_num].shape[1]
        total_sum = total_sum + jnp.pad(levels[level_num] * weights[level_num], ((0, 0), (0, padding), (0, 0)))
    return total_sum

def correct_block(state_block, levels, span_ticks, jac_rows, normal_rows, orient_rows, lame_first, shear_mod, inv_density, own_faces, gathered, top_speed, stiff_mats, lift_mats, orient_mats):
    own_integral = integrate(levels, time_weights(0, span_ticks))
    derived_vals = jnp.einsum('ab,qbe->qae', stiff_mats.reshape(3 * 56, 56), own_integral, precision=highest)
    volume = None
    for ref_dir in range(3):
        contrib = star_apply(jac_rows[ref_dir], derived_vals[:, ref_dir * 56:(ref_dir + 1) * 56, :], lame_first, shear_mod, inv_density)
        volume = contrib if volume is None else volume + contrib
    flux_list = []
    for face_num in range(4):
        outward = gathered[:, :, face_num, :]
        turned = jnp.einsum('hab,qbe->hqae', orient_mats, outward, precision=highest)
        orient_now = orient_rows[face_num]
        neighbour = jnp.where(orient_now == 0, turned[0], jnp.where(orient_now == 1, turned[1], turned[2]))
        inner_side = own_faces[:, :, face_num, :]
        flux_list.append(0.5 * star_apply(normal_rows[face_num], inner_side + neighbour, lame_first, shear_mod, inv_density) + 0.5 * top_speed * (inner_side - neighbour))
    fluxes = jnp.stack(flux_list, axis=1)
    lifted = jnp.einsum('fab,qfbe->qae', lift_mats, fluxes, precision=highest)
    return state_block + volume - lifted

def reference(dof_state, jacobian_inv, face_normals, material, deriv_mats, stiff_mats, trace_mats, lift_mats, orient_mats, nbr_slot, nbr_face, orient_code, send_list):
    starts = (0, BLK, 3 * BLK)
    widths = (BLK, 2 * BLK, 4 * BLK)

    def take_cluster(array, cluster):
        lead_dims = array.shape[:-1]
        by_device = array.reshape(lead_dims + (N_DOM, ELEMS))
        picked = by_device[..., starts[cluster]:starts[cluster] + widths[cluster]]
        return picked.reshape(lead_dims + (N_DOM * widths[cluster],))

    def assemble(pieces):
        lead_dims = pieces[0].shape[:-1]
        shaped = [pieces[cluster].reshape(lead_dims + (N_DOM, widths[cluster])) for cluster in range(3)]
        return jnp.concatenate(shaped, axis=-1).reshape(lead_dims + (MESH_ELEMS,))
    density, lame_all, shear_all = (material[0], material[1], material[2])
    inv_all = 1.0 / density
    top_speed = jnp.max(jnp.sqrt((lame_all + 2.0 * shear_all) * inv_all))
    device_of = jnp.arange(MESH_ELEMS, dtype=jnp.int32) // ELEMS
    shifted = nbr_slot - ELEMS
    peer_num = jnp.clip(shifted // (3 * CAPC), 0, PEERS - 1)
    clus_num = shifted // CAPC % 3
    slot_num = shifted % CAPC
    offset_of = jnp.array(peer_offsets, jnp.int32)[peer_num]
    sender = (device_of[None, :] - offset_of) % N_DOM
    entry = send_list[peer_num, clus_num, sender * CAPC + slot_num]
    remote_elem = sender * ELEMS + entry // 4
    local_elem = device_of[None, :] * ELEMS + nbr_slot
    source = jnp.where(nbr_slot < ELEMS, local_elem, remote_elem)
    src_col = (nbr_face * MESH_ELEMS + source).astype(jnp.int32)
    props = []
    for cluster in range(3):
        jac_rows = tuple((tuple((take_cluster(jacobian_inv[ref_dir, axis_num], cluster) for axis_num in range(3))) for ref_dir in range(3)))
        normal_rows = tuple((tuple((take_cluster(face_normals[face_num, axis_num], cluster) for axis_num in range(3))) for face_num in range(4)))
        props.append((jac_rows, normal_rows, take_cluster(orient_code, cluster), take_cluster(lame_all, cluster), take_cluster(shear_all, cluster), take_cluster(inv_all, cluster)))
    state_parts = [take_cluster(dof_state, cluster) for cluster in range(3)]
    levels_by = [None, None, None]
    begin_tick = [0, 0, 0]
    own_acc = [None, None, None]
    for tick_num in range(4):
        for cluster in range(3):
            if tick_num % 2 ** cluster == 0:
                jac_rows, normal_rows, orient_rows, lame_first, shear_mod, inv_density = props[cluster]
                levels_by[cluster] = taylor_levels(state_parts[cluster], deriv_mats, jac_rows, lame_first, shear_mod, inv_density)
                begin_tick[cluster] = tick_num
        tick_parts = []
        for cluster in range(3):
            offset_ticks = tick_num - begin_tick[cluster]
            tick_parts.append(integrate(levels_by[cluster], time_weights(offset_ticks, offset_ticks + 1)))
        tick_integral = assemble(tick_parts)
        tick_traces = jnp.einsum('fab,qbe->qafe', trace_mats, tick_integral, precision=highest).reshape(NQ * NF, 4 * MESH_ELEMS)
        for cluster in range(3):
            if tick_num % 2 ** cluster == 0:
                own_acc[cluster] = tick_traces
            else:
                own_acc[cluster] = own_acc[cluster] + tick_traces
        for cluster in range(3):
            if (tick_num + 1) % 2 ** cluster == 0:
                jac_rows, normal_rows, orient_rows, lame_first, shear_mod, inv_density = props[cluster]
                own_faces = take_cluster(own_acc[cluster].reshape(NQ, NF, 4, MESH_ELEMS), cluster)
                columns = take_cluster(src_col, cluster).reshape(-1)
                gathered = jnp.take(own_acc[cluster], columns, axis=1).reshape(NQ, NF, 4, N_DOM * widths[cluster])
                state_parts[cluster] = correct_block(state_parts[cluster], levels_by[cluster], 2 ** cluster, jac_rows, normal_rows, orient_rows, lame_first, shear_mod, inv_density, own_faces, gathered, top_speed, stiff_mats, lift_mats, orient_mats)
    return assemble(state_parts)
```

```python
import math

import jax
import jax.numpy as jnp
from jax import lax
from jax.experimental import pallas as pl
from jax.experimental.pallas import tpu as pltpu
from jax.sharding import PartitionSpec as P

NQ = 9
NB = 56
NF = 21
FR = 24
LANE = 128
TILES = 7
PEERS = 4
CAPC = 32
ELEMS = TILES * LANE
F32 = jnp.float32
BF16 = jnp.bfloat16

step_size = 0.04
peer_offsets = (-2, -1, 1, 2)
level_rows = (56, 40, 24, 16, 8, 8)
level_k = (64, 48, 32, 16, 16)
level_m = (128, 80, 48, 32, 32)
sizes = (56, 35, 20, 10, 4, 1)
STIFF_M = 272
ROWS = NQ * FR
PACK = 56


def time_weights(lower, upper):
    return [
        step_size ** (k + 1) * (upper ** (k + 1) - lower ** (k + 1)) / math.factorial(k + 1)
        for k in range(6)
    ]


def split3(a):
    hi = lax.reduce_precision(a, 8, 7)
    lo = lax.reduce_precision(a - hi, 8, 7)
    return jnp.concatenate([hi, hi, lo], axis=1).astype(BF16)


def pad2(a, rows, cols):
    return jnp.pad(a, ((0, rows - a.shape[0]), (0, cols - a.shape[1])))


def prepare(deriv_mats, stiff_mats, trace_mats, lift_mats, orient_mats):
    mats = []
    for k in range(5):
        n_in, n_out = sizes[k], sizes[k + 1]
        blocks = [
            pad2(deriv_mats[xi, :n_out, :n_in], level_rows[k + 1], level_k[k]) for xi in range(3)
        ]
        mats.append(split3(pad2(jnp.concatenate(blocks, axis=0), level_m[k], level_k[k])))
    trace = jnp.concatenate([pad2(trace_mats[f], FR, 64) for f in range(4)], axis=0)
    stiff = pad2(stiff_mats.reshape(3 * NB, NB), 3 * NB, 64)
    mats.append(split3(pad2(jnp.concatenate([stiff, trace], axis=0), STIFF_M, 64)))
    mats.append(split3(trace))
    turn = jnp.concatenate([pad2(orient_mats[h], FR, 32) for h in range(3)], axis=0)
    mats.append(split3(pad2(turn, 80, 32)))
    lift = jnp.concatenate([pad2(lift_mats[f], 64, FR) for f in range(4)], axis=1)
    mats.append(split3(lift))
    return mats


def hi_lo(x):
    hi = x.astype(BF16)
    return hi, (x - hi.astype(F32)).astype(BF16)


def kernel(
    n_dev,
    top_ref,
    state_in,
    jac_ref,
    nrm_ref,
    mat_ref,
    m0,
    m1,
    m2,
    m3,
    m4,
    m_stiff,
    m_trace,
    m_orient,
    m_lift,
    slot_ref,
    face_ref,
    code_ref,
    send_ref,
    out_ref,
    coef,
    tabs,
    onehot,
    onehot_send,
    onehot_ghost,
    meta,
    meta_send,
    own,
    seen,
    gath,
    der,
    x3,
    lv1,
    lv2,
    lv3,
    lv4,
    lv5,
    acc,
    fl,
    x_lift,
    ghost,
    sbuf,
    rbuf,
    send_sem,
    recv_sem,
):
    me = lax.axis_index("dom")
    targets = [lax.rem(me + n_dev + off, n_dev) for off in peer_offsets]
    level_mats = (m0, m1, m2, m3, m4)
    level_refs = (None, lv1, lv2, lv3, lv4, lv5)
    barrier = pltpu.get_barrier_semaphore()
    for dev in targets:
        pl.semaphore_signal(barrier, inc=1, device_id=(dev,), device_id_type=pl.DeviceIdType.MESH)

    half_top = 0.5 * top_ref[0, 0]
    out_ref[...] = state_in[...]
    mat = mat_ref[...]
    inv_rho = 1.0 / mat[0:1]
    rows = [jac_ref[xi][j : j + 1] for xi in range(3) for j in range(3)]
    rows += [nrm_ref[f][j : j + 1] for f in range(4) for j in range(3)]
    rows += [mat[1:2], 2.0 * mat[2:3], mat[2:3], inv_rho]
    for t in range(TILES):
        for i, row in enumerate(rows):
            coef[t, i] = jnp.broadcast_to(row[:, t * LANE : (t + 1) * LANE], (8, LANE))

    slots = slot_ref[...]
    faces = face_ref[...]
    codes = code_ref[...]
    away = slots - ELEMS
    peer = (
        (away >= 96).astype(jnp.int32)
        + (away >= 192).astype(jnp.int32)
        + (away >= 288).astype(jnp.int32)
    )
    ghost_col = jnp.where(away >= 0, peer * CAPC + (away & (CAPC - 1)), -1)
    elem_rows = lax.broadcasted_iota(jnp.int32, (ELEMS, LANE), 0)
    ghost_rows = lax.broadcasted_iota(jnp.int32, (LANE, LANE), 0)

    def hot(rows_iota, line):
        return jnp.where(rows_iota == line, 1.0, 0.0).astype(BF16)

    for t in range(TILES):
        for f in range(4):
            cut = slice(t * LANE, (t + 1) * LANE)
            at = slice(f * LANE, (f + 1) * LANE)
            onehot[t, :, at] = hot(elem_rows, slots[f : f + 1, cut])
            g = hot(ghost_rows, ghost_col[f : f + 1, cut])
            onehot_ghost[t, 0:LANE, at] = g
            onehot_ghost[t, LANE : 2 * LANE, at] = g
            meta[t, 0, :, at] = jnp.broadcast_to(faces[f : f + 1, cut], (8, LANE))
            meta[t, 1, :, at] = jnp.broadcast_to(codes[f : f + 1, cut], (8, LANE))
    sends = send_ref[...]
    send_elem = jnp.where(sends >= 0, sends >> 2, -1)
    send_face = sends & 3
    for c in range(3):
        onehot_send[c] = hot(elem_rows, send_elem[c : c + 1])
        meta_send[c] = jnp.broadcast_to(send_face[c : c + 1], (8, LANE))

    pl.semaphore_wait(barrier, PEERS)


    def star_rows(c, read):
        n_xi = len(c)

        def total(pairs):
            out = None
            for xi in range(n_xi):
                for j, q in pairs:
                    term = c[xi][j] * vals[xi][q]
                    out = term if out is None else out + term
            return out

        vals = [[read(xi, q) for q in range(NQ)] for xi in range(n_xi)]
        return total

    def star(c, lam, mu2, mu, irho, read):
        total = star_rows(c, read)
        p = total([(0, 6)])
        q = total([(1, 7)])
        r = total([(2, 8)])
        div = lam * (p + q + r)
        return [
            div + mu2 * p,
            div + mu2 * q,
            div + mu2 * r,
            mu * total([(1, 6), (0, 7)]),
            mu * total([(2, 7), (1, 8)]),
            mu * total([(2, 6), (0, 8)]),
            irho * total([(0, 0), (1, 3), (2, 5)]),
            irho * total([(0, 3), (1, 1), (2, 4)]),
            irho * total([(0, 5), (1, 4), (2, 2)]),
        ]

    def store_split(ref, row, col, k_pad, x, width):
        hi, lo = hi_lo(x)
        ref[row : row + 16, col : col + width] = hi
        ref[k_pad + row : k_pad + row + 16, col : col + width] = lo
        ref[2 * k_pad + row : 2 * k_pad + row + 16, col : col + width] = hi

    def put_operand(ref, k_pad, q, pieces):
        if len(pieces) % 2:
            pieces = pieces + [jnp.zeros((8, LANE), F32)]
        for i in range(0, len(pieces), 2):
            pair = jnp.concatenate([pieces[i], pieces[i + 1]], axis=0)
            store_split(ref, i * 8, q * LANE, k_pad, pair, LANE)

    def predict(tile, table_of, weights):
        base = pl.multiple_of(tile * LANE, LANE)
        lanes = pl.ds(base, LANE)
        cj = [[coef[tile, 3 * xi + j] for j in range(3)] for xi in range(3)]
        lam, mu2, mu, irho = [coef[tile, 21 + i] for i in range(4)]
        for q in range(NQ):
            put_operand(x3, 64, q, [out_ref[q, r * 8 : r * 8 + 8, lanes] for r in range(7)])
        for k in range(5):
            kp = level_k[k]
            m = level_m[k]
            der[0:m, :] = jnp.dot(
                level_mats[k][...], x3[0 : 3 * kp, :], preferred_element_type=F32
            )
            n = level_rows[k + 1]
            pend = [[] for _ in range(NQ)]
            for r in range(n // 8):

                def read(xi, q, r=r):
                    lo_row = xi * n + r * 8
                    return der[lo_row : lo_row + 8, q * LANE : (q + 1) * LANE]

                vals = star(cj, lam, mu2, mu, irho, read)
                for q in range(NQ):
                    level_refs[k + 1][q, r * 8 : r * 8 + 8, :] = vals[q]
                    pend[q].append(vals[q])
                last = r == n // 8 - 1
                if k < 4 and (r % 2 == 1 or last):
                    for q in range(NQ):
                        lo_piece = pend[q][0]
                        hi_piece = pend[q][1] if len(pend[q]) == 2 else jnp.zeros((8, LANE), F32)
                        pair = jnp.concatenate([lo_piece, hi_piece], axis=0)
                        store_split(x3, (r // 2) * 16, q * LANE, level_k[k + 1], pair, LANE)
                if r % 2 == 1 or last:
                    pend = [[] for _ in range(NQ)]
        own_pend = [[] for _ in range(NQ)]
        held = {}
        for v in range(64):
            if v < 63:
                q, r = divmod(v, 7)
                terms = [out_ref[q, r * 8 : r * 8 + 8, lanes]]
                for k in range(1, 6):
                    if r * 8 < level_rows[k]:
                        terms.append(level_refs[k][q, r * 8 : r * 8 + 8, :])
                ticks = []
                for w in weights:
                    total = terms[0] * w[0]
                    for k in range(1, len(terms)):
                        total = total + terms[k] * w[k]
                    ticks.append(total)
                entries, own_int = table_of(v, ticks)
                own_pend[q].append(own_int)
                if r == 6:
                    put_operand(x3, 64, q, own_pend[q])
            else:
                entries = [(idx, jnp.zeros((8, LANE), F32)) for idx, _ in entries]
            if v % 2 == 0:
                held = entries
            else:
                for (idx, first), (_, second) in zip(held, entries):
                    hi, lo = hi_lo(jnp.concatenate([first, second], axis=0))
                    row = (v // 2) * 16
                    tabs[idx, row : row + 16, lanes] = hi
                    tabs[idx, 512 + row : 512 + row + 16, lanes] = lo
        der[...] = jnp.dot(m_stiff[...], x3[...], preferred_element_type=F32)
        for r in range(7):

            def read(xi, q, r=r):
                lo_row = xi * NB + r * 8
                return der[lo_row : lo_row + 8, q * LANE : (q + 1) * LANE]

            vals = star(cj, lam, mu2, mu, irho, read)
            for q in range(NQ):
                out_ref[q, r * 8 : r * 8 + 8, lanes] = (
                    out_ref[q, r * 8 : r * 8 + 8, lanes] - vals[q]
                )
        own[tile] = der[168 : 168 + 96, :]

    def gather_traces(table, hot_mat, face_rows, width, put):
        gath[:, 0:width] = jnp.dot(tabs[table], hot_mat, preferred_element_type=F32)
        is_one, is_two, is_three = [
            jnp.concatenate([face_rows == i] * 3, axis=0) for i in (1, 2, 3)
        ]
        zero = jnp.zeros((8, width), F32)
        for q in range(NQ):
            hi = jnp.concatenate([gath[q * NB : (q + 1) * NB, 0:width], zero], axis=0).astype(BF16)
            lo = jnp.concatenate(
                [gath[512 + q * NB : 512 + (q + 1) * NB, 0:width], zero], axis=0
            ).astype(BF16)
            x = jnp.concatenate([hi, lo, hi], axis=0)
            t = jnp.dot(m_trace[...], x, preferred_element_type=F32)
            pick = jnp.where(
                is_three,
                t[3 * FR : 4 * FR],
                jnp.where(
                    is_two, t[2 * FR : 3 * FR], jnp.where(is_one, t[FR : 2 * FR], t[0:FR])
                ),
            )
            put(q, pick)

    lane_group = lax.broadcasted_iota(jnp.int32, (PACK, LANE), 1) // CAPC

    def transpose_blocks(read):
        outs = []
        blocks = [read(g) for g in range(4)]
        for p in range(4):
            out = None
            for g in range(4):
                shift = ((g - p) * CAPC) % LANE
                turned = pltpu.roll(blocks[g], shift, 1) if shift else blocks[g]
                out = turned if out is None else jnp.where(lane_group == g, turned, out)
            outs.append(out)
        return outs

    def copies(combo):
        return [
            pltpu.make_async_remote_copy(
                src_ref=sbuf.at[combo, p],
                dst_ref=rbuf.at[combo, p],
                send_sem=send_sem.at[combo, p],
                recv_sem=recv_sem.at[combo, p],
                device_id=(targets[p],),
                device_id_type=pl.DeviceIdType.MESH,
            )
            for p in range(PEERS)
        ]

    def send_cluster(c, combo):
        def put(q, pick):
            ghost_stage[q * FR : (q + 1) * FR, :] = pick

        ghost_stage = fl.at[0 : 4 * PACK, 0:LANE]
        ghost_stage[ROWS : 4 * PACK, :] = jnp.zeros((4 * PACK - ROWS, LANE), F32)
        gather_traces(combo, onehot_send[c], meta_send[c], LANE, put)
        outs = transpose_blocks(lambda g: ghost_stage[g * PACK : (g + 1) * PACK, :])
        for p in range(PEERS):
            sbuf[combo, p] = outs[p]
        for copy in copies(combo):
            copy.start()

    def gather_tile(tile, table):
        def put(q, pick):
            seen[tile, q * FR : (q + 1) * FR, :] = pick

        gather_traces(table, onehot[tile], meta[tile, 0], 4 * LANE, put)

    def receive_cluster(c, combo):
        for copy in copies(combo):
            copy.wait()
        outs = transpose_blocks(lambda p: rbuf[combo, p])
        full = jnp.concatenate(outs, axis=0)
        hi, lo = hi_lo(full)
        ghost[c, :, 0:LANE] = hi
        ghost[c, :, LANE : 2 * LANE] = lo

    def correct_tile(tile, c):
        base = pl.multiple_of(tile * LANE, LANE)
        lanes = pl.ds(base, LANE)
        gath[0 : 4 * PACK, :] = jnp.dot(
            ghost[c], onehot_ghost[tile], preferred_element_type=F32
        )
        code = meta[tile, 1]
        is_one, is_two = [jnp.concatenate([code == i] * 3, axis=0) for i in (1, 2)]
        zero = jnp.zeros((8, 4 * LANE), F32)
        for q in range(NQ):
            cut = slice(q * FR, (q + 1) * FR)
            arrived = seen[tile, cut, :] + gath[cut, :]
            hi, lo = hi_lo(jnp.concatenate([arrived, zero], axis=0))
            x = jnp.concatenate([hi, lo, hi], axis=0)
            t = jnp.dot(m_orient[...], x, preferred_element_type=F32)
            seen[tile, cut, :] = jnp.where(
                is_two, t[2 * FR : 3 * FR], jnp.where(is_one, t[FR : 2 * FR], t[0:FR])
            )
        lam, mu2, mu, irho = [-0.5 * coef[tile, 21 + i] for i in range(4)]
        for f in range(4):
            normal = [[coef[tile, 9 + 3 * f + j] for j in range(3)]]
            for r in range(3):
                inner = [
                    own[tile, f * FR + r * 8 : f * FR + r * 8 + 8, q * LANE : (q + 1) * LANE]
                    for q in range(NQ)
                ]
                outer = [
                    seen[
                        tile, q * FR + r * 8 : q * FR + r * 8 + 8, f * LANE : (f + 1) * LANE
                    ]
                    for q in range(NQ)
                ]
                both = [a + b for a, b in zip(inner, outer)]
                vals = star(normal, lam, mu2, mu, irho, lambda xi, q: both[q])
                for q in range(NQ):
                    row = f * FR + r * 8
                    fl[row : row + 8, q * LANE : (q + 1) * LANE] = vals[q] + half_top * (
                        inner[q] - outer[q]
                    )
        for i in range(6):
            for q in range(NQ):
                col = q * LANE
                store_split(
                    x_lift, i * 16, col, 96, fl[i * 16 : i * 16 + 16, col : col + LANE], LANE
                )
        der[0:64, :] = jnp.dot(m_lift[...], x_lift[...], preferred_element_type=F32)
        for q in range(NQ):
            out_ref[q, :, lanes] = out_ref[q, :, lanes] - der[0:NB, q * LANE : (q + 1) * LANE]


    acc[...] = jnp.zeros_like(acc)
    w_tick = [time_weights(i, i + 1) for i in range(4)]

    def tables_2(v, ticks):
        j0, j1, j2, j3 = ticks
        first, second = j0 + j1, j2 + j3
        whole = first + second
        return [(0, j0), (1, j1), (2, j2), (3, j3), (4, first), (5, second), (6, whole)], whole

    def predict_2(i, carry):
        predict(3 + i, tables_2, w_tick)
        return carry

    lax.fori_loop(0, 4, predict_2, 0)

    def tick(t, carry):
        half = t // 2
        odd = t - 2 * half
        last = t // 3

        @pl.when(odd == 0)
        def _():
            def tables_1(v, ticks):
                j0, j1 = ticks
                pair = j0 + j1
                return [(t, j0), (t + 1, j1), (4 + half, pair)], pair

            def tables_1_all(i):
                def inner(v, ticks):
                    entries, pair = tables_1(v, ticks)
                    whole = pair + acc[2 + i, v * 8 : v * 8 + 8, :]
                    acc[2 + i, v * 8 : v * 8 + 8, :] = whole
                    return entries + [(6, whole)], pair

                return inner

            def predict_1(i, carry):
                predict(1 + i, tables_1_all(i), w_tick[:2])
                return carry

            lax.fori_loop(0, 2, predict_1, 0)

        keep = (1 - odd).astype(F32)

        def tables_0(v, ticks):
            (j0,) = ticks
            rows_v = slice(v * 8, v * 8 + 8)
            pair = j0 + acc[0, rows_v, :]
            acc[0, rows_v, :] = pair * keep
            whole = j0 + acc[1, rows_v, :]
            acc[1, rows_v, :] = whole
            return [(t, j0), (4 + half, pair), (6, whole)], j0

        predict(0, tables_0, w_tick[:1])

        n_due = 1 + odd + last
        n_tiles = 1 + 2 * odd + 4 * last

        def combo_of(a, b):
            return (1 - a) * t + (a - b) * (4 + half) + b * 6

        def send_step(c, carry):
            a = (c + 1) // 2
            b = c // 2
            send_cluster(c, combo_of(a, b))
            return carry

        def gather_step(j, carry):
            a = (j + 6) // 7
            b = (j + 4) // 7
            gather_tile(j, combo_of(a, b))
            return carry

        def receive_step(c, carry):
            a = (c + 1) // 2
            b = c // 2
            receive_cluster(c, combo_of(a, b))
            return carry

        def correct_step(j, carry):
            correct_tile(j, (j + 6) // 7 + (j + 4) // 7)
            return carry

        lax.fori_loop(0, n_due, send_step, 0)
        lax.fori_loop(0, n_tiles, gather_step, 0)
        lax.fori_loop(0, n_due, receive_step, 0)
        lax.fori_loop(0, n_tiles, correct_step, 0)
        return carry

    lax.fori_loop(0, 4, tick, 0)


def local(
    dof_state,
    jacobian_inv,
    face_normals,
    material,
    deriv_mats,
    stiff_mats,
    trace_mats,
    lift_mats,
    orient_mats,
    nbr_slot,
    nbr_face,
    orient_code,
    send_list,
):
    n_dev = lax.axis_size("dom")
    top = jnp.max(jnp.sqrt((material[1] + 2.0 * material[2]) * (1.0 / material[0])))
    top = lax.pmax(top, "dom").reshape(1, 1)
    mats = prepare(deriv_mats, stiff_mats, trace_mats, lift_mats, orient_mats)
    sends = jnp.transpose(send_list, (1, 0, 2)).reshape(3, LANE)
    vmem = pl.BlockSpec(memory_space=pltpu.VMEM)

    def run(*refs):
        kernel(n_dev, *refs)

    return pl.pallas_call(
        run,
        out_shape=jax.ShapeDtypeStruct((NQ, NB, ELEMS), F32),
        in_specs=[pl.BlockSpec(memory_space=pltpu.SMEM)] + [vmem] * 17,
        out_specs=vmem,
        scratch_shapes=[
            pltpu.VMEM((TILES, 25, 8, LANE), F32),
            pltpu.VMEM((7, 1024, ELEMS), BF16),
            pltpu.VMEM((TILES, ELEMS, 4 * LANE), BF16),
            pltpu.VMEM((3, ELEMS, LANE), BF16),
            pltpu.VMEM((TILES, 2 * LANE, 4 * LANE), BF16),
            pltpu.VMEM((TILES, 2, 8, 4 * LANE), jnp.int32),
            pltpu.VMEM((3, 8, LANE), jnp.int32),
            pltpu.VMEM((TILES, 96, NQ * LANE), F32),
            pltpu.VMEM((TILES, ROWS, 4 * LANE), F32),
            pltpu.VMEM((1024, 4 * LANE), F32),
            pltpu.VMEM((STIFF_M, NQ * LANE), F32),
            pltpu.VMEM((192, NQ * LANE), BF16),
            pltpu.VMEM((NQ, 40, LANE), F32),
            pltpu.VMEM((NQ, 24, LANE), F32),
            pltpu.VMEM((NQ, 16, LANE), F32),
            pltpu.VMEM((NQ, 8, LANE), F32),
            pltpu.VMEM((NQ, 8, LANE), F32),
            pltpu.VMEM((4, NQ * NB, LANE), F32),
            pltpu.VMEM((4 * PACK, NQ * LANE), F32),
            pltpu.VMEM((288, NQ * LANE), BF16),
            pltpu.VMEM((3, 4 * PACK, 2 * LANE), BF16),
            pltpu.VMEM((7, PEERS, PACK, LANE), F32),
            pltpu.VMEM((7, PEERS, PACK, LANE), F32),
            pltpu.SemaphoreType.DMA((7, PEERS)),
            pltpu.SemaphoreType.DMA((7, PEERS)),
        ],
        compiler_params=pltpu.CompilerParams(
            collective_id=0, has_side_effects=True, vmem_limit_bytes=58 * 1024 * 1024
        ),
        cost_estimate=pl.CostEstimate(
            flops=25_000_000_000, bytes_accessed=6_000_000, transcendentals=0
        ),
    )(
        top,
        dof_state,
        jacobian_inv,
        face_normals,
        material,
        *mats,
        nbr_slot,
        nbr_face,
        orient_code,
        sends,
    )


def solution(mesh):
    return jax.shard_map(
        local,
        mesh=mesh,
        in_specs=(
            P(None, None, "dom"),
            P(None, None, "dom"),
            P(None, None, "dom"),
            P(None, "dom"),
            P(),
            P(),
            P(),
            P(),
            P(),
            P(None, "dom"),
            P(None, "dom"),
            P(None, "dom"),
            P(None, None, "dom"),
        ),
        out_specs=P(None, None, "dom"),
        check_vma=False,
    )
```

```python
import math

import jax
import jax.numpy as jnp
from jax import lax
from jax.experimental import pallas as pl
from jax.experimental.pallas import tpu as pltpu
from jax.sharding import PartitionSpec as P

NQ = 9
NB = 56
NF = 21
FR = 24
LANE = 128
TILES = 7
PEERS = 4
CAPC = 32
ELEMS = TILES * LANE
F32 = jnp.float32
BF16 = jnp.bfloat16

step_size = 0.04
peer_offsets = (-2, -1, 1, 2)
level_rows = (56, 40, 24, 16, 8, 8)
level_k = (64, 48, 32, 16, 16)
level_m = (128, 80, 48, 32, 32)
sizes = (56, 35, 20, 10, 4, 1)
STIFF_M = 272
ROWS = NQ * FR
PACK = 56


def time_weights(lower, upper):
    return [
        step_size ** (k + 1) * (upper ** (k + 1) - lower ** (k + 1)) / math.factorial(k + 1)
        for k in range(6)
    ]


def hi_lo(x):
    hi = x.astype(BF16)
    return hi, (x - hi.astype(F32)).astype(BF16)


def kernel(
    n_dev,
    radices,
    state_in,
    jac_ref,
    nrm_ref,
    mat_ref,
    deriv_ref,
    stiff_ref,
    trace_ref,
    lift_ref,
    orient_ref,
    slot_ref,
    face_ref,
    code_ref,
    send_ref,
    out_ref,
    m0,
    m1,
    m2,
    m3,
    m4,
    m_stiff,
    m_trace,
    m_orient,
    m_lift,
    stage,
    send_stage,
    top_out,
    top_in,
    top_send_sem,
    top_recv_sem,
    coef,
    tabs,
    onehot,
    onehot_send,
    onehot_ghost,
    meta,
    meta_send,
    own,
    seen,
    gath,
    der,
    x3,
    lv1,
    lv2,
    lv3,
    lv4,
    lv5,
    acc,
    fl,
    x_lift,
    ghost,
    sbuf,
    rbuf,
    send_sem,
    recv_sem,
):
    me = lax.axis_index("dom")
    targets = [lax.rem(me + n_dev + off, n_dev) for off in peer_offsets]
    level_mats = (m0, m1, m2, m3, m4)
    level_refs = (None, lv1, lv2, lv3, lv4, lv5)
    partners = []
    stride = 1
    for radix in radices:
        place = lax.rem(me // stride, radix)
        partners.append(
            [me + (lax.rem(place + i, radix) - place) * stride for i in range(1, radix)]
        )
        stride *= radix
    greeted = targets + [dev for group in partners for dev in group]
    barrier = pltpu.get_barrier_semaphore()
    for dev in greeted:
        pl.semaphore_signal(barrier, inc=1, device_id=(dev,), device_id_type=pl.DeviceIdType.MESH)

    mat = mat_ref[...]
    inv_rho = 1.0 / mat[0:1]
    speed = jnp.sqrt((mat[1:2] + 2.0 * mat[2:3]) * inv_rho)
    top_out[0] = jnp.broadcast_to(jnp.max(speed, axis=1, keepdims=True), (8, LANE))

    def top_copies(level):
        return [
            pltpu.make_async_remote_copy(
                src_ref=top_out.at[level],
                dst_ref=top_in.at[level, i],
                send_sem=top_send_sem.at[level, i],
                recv_sem=top_recv_sem.at[level, i],
                device_id=(dev,),
                device_id_type=pl.DeviceIdType.MESH,
            )
            for i, dev in enumerate(partners[level])
        ]

    def top_start(level):
        for copy in top_copies(level):
            copy.start()

    def top_finish(level):
        for copy in top_copies(level):
            copy.wait()
        best = top_out[level]
        for i in range(len(partners[level])):
            best = jnp.maximum(best, top_in[level, i])
        top_out[level + 1] = best

    n_levels = len(radices)
    lane_of = lax.broadcasted_iota(jnp.int32, (stage.shape[0], LANE), 1)

    def lay(m_ref, rows, k_pad, base):
        hi = base.astype(BF16).astype(F32)
        lo = base - hi
        cols = [None] * (m_ref.shape[1] // LANE)
        for i, part in enumerate((hi, hi, lo)):
            at = i * k_pad
            col, off = divmod(at, LANE)
            turned = pltpu.roll(part, off, 1) if off else part
            if off + k_pad <= LANE:
                pieces = [(col, turned)]
            else:
                wide = lane_of[0:rows] >= off
                pieces = [(col, jnp.where(wide, turned, 0.0)), (col + 1, jnp.where(wide, 0.0, turned))]
            for c, piece in pieces:
                cols[c] = piece if cols[c] is None else cols[c] + piece
        for c, piece in enumerate(cols):
            m_ref[:, c * LANE : (c + 1) * LANE] = piece.astype(BF16)

    def clear():
        stage[...] = jnp.zeros_like(stage)

    for k, m_ref in enumerate(level_mats):
        n_in, n_out = sizes[k], sizes[k + 1]
        clear()
        for xi in range(3):
            row = xi * level_rows[k + 1]
            stage[row : row + n_out, 0:n_in] = deriv_ref[xi, 0:n_out, 0:n_in]
        lay(m_ref, level_m[k], level_k[k], stage[0 : level_m[k], :])
    clear()
    for xi in range(3):
        stage[xi * NB : (xi + 1) * NB, 0:NB] = stiff_ref[xi]
    for f in range(4):
        row = 3 * NB + f * FR
        stage[row : row + NF, 0:NB] = trace_ref[:, f, :]
    lay(m_stiff, STIFF_M, 64, stage[0:STIFF_M, :])
    lay(m_trace, 96, 64, stage[3 * NB : 3 * NB + 96, :])
    clear()
    for h in range(3):
        stage[h * FR : h * FR + NF, 0:NF] = orient_ref[h]
    lay(m_orient, 80, 32, stage[0:80, :])
    clear()
    for f in range(4):
        stage[f * FR : f * FR + NF, 0:NB] = lift_ref[:, f, :]
    lay(m_lift, 64, 96, jnp.transpose(stage[0:LANE, :])[0:64, :])

    out_ref[...] = state_in[...]
    pl.semaphore_wait(barrier, len(greeted))
    top_start(0)
    rows = [jac_ref[xi][j : j + 1] for xi in range(3) for j in range(3)]
    rows += [nrm_ref[j][f : f + 1] for f in range(4) for j in range(3)]
    rows += [mat[1:2], 2.0 * mat[2:3], mat[2:3], inv_rho]
    for t in range(TILES):
        for i, row in enumerate(rows):
            coef[t, i] = jnp.broadcast_to(row[:, t * LANE : (t + 1) * LANE], (8, LANE))

    slots = slot_ref[...]
    faces = face_ref[...]
    codes = code_ref[...]
    away = slots - ELEMS
    peer = (
        (away >= 96).astype(jnp.int32)
        + (away >= 192).astype(jnp.int32)
        + (away >= 288).astype(jnp.int32)
    )
    ghost_col = jnp.where(away >= 0, peer * CAPC + (away & (CAPC - 1)), -1)
    elem_rows = lax.broadcasted_iota(jnp.int32, (ELEMS, LANE), 0)
    ghost_rows = lax.broadcasted_iota(jnp.int32, (LANE, LANE), 0)

    def hot(rows_iota, line):
        return jnp.where(rows_iota == line, 1.0, 0.0).astype(BF16)

    for t in range(TILES):
        if t == 3 and n_levels > 1:
            top_finish(0)
            top_start(1)
        for f in range(4):
            cut = slice(t * LANE, (t + 1) * LANE)
            at = slice(f * LANE, (f + 1) * LANE)
            onehot[t, :, at] = hot(elem_rows, slots[f : f + 1, cut])
            g = hot(ghost_rows, ghost_col[f : f + 1, cut])
            onehot_ghost[t, 0:LANE, at] = g
            onehot_ghost[t, LANE : 2 * LANE, at] = g
            meta[t, 0, :, at] = jnp.broadcast_to(faces[f : f + 1, cut], (8, LANE))
            meta[t, 1, :, at] = jnp.broadcast_to(codes[f : f + 1, cut], (8, LANE))
    send_stage[...] = jnp.zeros_like(send_stage)
    send_lane = lax.broadcasted_iota(jnp.int32, (1, LANE), 1) // CAPC
    for c in range(3):
        send_stage[c, 0:PEERS, 0:CAPC] = send_ref[c]
    lines = []
    for c in range(3):
        line = send_stage[c, 0:1, :]
        for p in range(1, PEERS):
            turned = pltpu.roll(send_stage[c], p * CAPC, 1)[p : p + 1]
            line = jnp.where(send_lane == p, turned, line)
        lines.append(line)
    for c in range(3):
        onehot_send[c] = hot(elem_rows, jnp.where(lines[c] >= 0, lines[c] >> 2, -1))
        meta_send[c] = jnp.broadcast_to(lines[c] & 3, (8, LANE))


    def star_rows(c, read):
        n_xi = len(c)

        def total(pairs):
            out = None
            for xi in range(n_xi):
                for j, q in pairs:
                    term = c[xi][j] * vals[xi][q]
                    out = term if out is None else out + term
            return out

        vals = [[read(xi, q) for q in range(NQ)] for xi in range(n_xi)]
        return total

    def star(c, lam, mu2, mu, irho, read):
        total = star_rows(c, read)
        p = total([(0, 6)])
        q = total([(1, 7)])
        r = total([(2, 8)])
        div = lam * (p + q + r)
        return [
            div + mu2 * p,
            div + mu2 * q,
            div + mu2 * r,
            mu * total([(1, 6), (0, 7)]),
            mu * total([(2, 7), (1, 8)]),
            mu * total([(2, 6), (0, 8)]),
            irho * total([(0, 0), (1, 3), (2, 5)]),
            irho * total([(0, 3), (1, 1), (2, 4)]),
            irho * total([(0, 5), (1, 4), (2, 2)]),
        ]

    def store_split(ref, row, col, k_pad, x, width):
        hi, lo = hi_lo(x)
        ref[row : row + 16, col : col + width] = hi
        ref[k_pad + row : k_pad + row + 16, col : col + width] = lo
        ref[2 * k_pad + row : 2 * k_pad + row + 16, col : col + width] = hi

    def put_operand(ref, k_pad, q, pieces):
        if len(pieces) % 2:
            pieces = pieces + [jnp.zeros((8, LANE), F32)]
        for i in range(0, len(pieces), 2):
            pair = jnp.concatenate([pieces[i], pieces[i + 1]], axis=0)
            store_split(ref, i * 8, q * LANE, k_pad, pair, LANE)

    def predict(tile, table_of, weights):
        base = pl.multiple_of(tile * LANE, LANE)
        lanes = pl.ds(base, LANE)
        cj = [[coef[tile, 3 * xi + j] for j in range(3)] for xi in range(3)]
        lam, mu2, mu, irho = [coef[tile, 21 + i] for i in range(4)]
        for q in range(NQ):
            put_operand(x3, 64, q, [out_ref[q, r * 8 : r * 8 + 8, lanes] for r in range(7)])
        for k in range(5):
            kp = level_k[k]
            m = level_m[k]
            der[0:m, :] = jnp.dot(
                level_mats[k][:, 0 : 3 * kp], x3[0 : 3 * kp, :], preferred_element_type=F32
            )
            n = level_rows[k + 1]
            pend = [[] for _ in range(NQ)]
            for r in range(n // 8):

                def read(xi, q, r=r):
                    lo_row = xi * n + r * 8
                    return der[lo_row : lo_row + 8, q * LANE : (q + 1) * LANE]

                vals = star(cj, lam, mu2, mu, irho, read)
                for q in range(NQ):
                    level_refs[k + 1][q, r * 8 : r * 8 + 8, :] = vals[q]
                    pend[q].append(vals[q])
                last = r == n // 8 - 1
                if k < 4 and (r % 2 == 1 or last):
                    for q in range(NQ):
                        lo_piece = pend[q][0]
                        hi_piece = pend[q][1] if len(pend[q]) == 2 else jnp.zeros((8, LANE), F32)
                        pair = jnp.concatenate([lo_piece, hi_piece], axis=0)
                        store_split(x3, (r // 2) * 16, q * LANE, level_k[k + 1], pair, LANE)
                if r % 2 == 1 or last:
                    pend = [[] for _ in range(NQ)]
        own_pend = [[] for _ in range(NQ)]
        held = {}
        for v in range(64):
            if v < 63:
                q, r = divmod(v, 7)
                terms = [out_ref[q, r * 8 : r * 8 + 8, lanes]]
                for k in range(1, 6):
                    if r * 8 < level_rows[k]:
                        terms.append(level_refs[k][q, r * 8 : r * 8 + 8, :])
                ticks = []
                for w in weights:
                    total = terms[0] * w[0]
                    for k in range(1, len(terms)):
                        total = total + terms[k] * w[k]
                    ticks.append(total)
                entries, own_int = table_of(v, ticks)
                own_pend[q].append(own_int)
                if r == 6:
                    put_operand(x3, 64, q, own_pend[q])
            else:
                entries = [(idx, jnp.zeros((8, LANE), F32)) for idx, _ in entries]
            if v % 2 == 0:
                held = entries
            else:
                for (idx, first), (_, second) in zip(held, entries):
                    hi, lo = hi_lo(jnp.concatenate([first, second], axis=0))
                    row = (v // 2) * 16
                    tabs[idx, row : row + 16, lanes] = hi
                    tabs[idx, 512 + row : 512 + row + 16, lanes] = lo
        der[...] = jnp.dot(m_stiff[:, 0:192], x3[...], preferred_element_type=F32)
        for r in range(7):

            def read(xi, q, r=r):
                lo_row = xi * NB + r * 8
                return der[lo_row : lo_row + 8, q * LANE : (q + 1) * LANE]

            vals = star(cj, lam, mu2, mu, irho, read)
            for q in range(NQ):
                out_ref[q, r * 8 : r * 8 + 8, lanes] = (
                    out_ref[q, r * 8 : r * 8 + 8, lanes] - vals[q]
                )
        own[tile] = der[168 : 168 + 96, :]

    def gather_traces(table, hot_mat, face_rows, width, put):
        gath[:, 0:width] = jnp.dot(tabs[table], hot_mat, preferred_element_type=F32)
        is_one, is_two, is_three = [
            jnp.concatenate([face_rows == i] * 3, axis=0) for i in (1, 2, 3)
        ]
        zero = jnp.zeros((8, width), F32)
        for q in range(NQ):
            hi = jnp.concatenate([gath[q * NB : (q + 1) * NB, 0:width], zero], axis=0).astype(BF16)
            lo = jnp.concatenate(
                [gath[512 + q * NB : 512 + (q + 1) * NB, 0:width], zero], axis=0
            ).astype(BF16)
            x = jnp.concatenate([hi, lo, hi], axis=0)
            t = jnp.dot(m_trace[:, 0:192], x, preferred_element_type=F32)
            pick = jnp.where(
                is_three,
                t[3 * FR : 4 * FR],
                jnp.where(
                    is_two, t[2 * FR : 3 * FR], jnp.where(is_one, t[FR : 2 * FR], t[0:FR])
                ),
            )
            put(q, pick)

    lane_group = lax.broadcasted_iota(jnp.int32, (PACK, LANE), 1) // CAPC

    def transpose_blocks(read):
        outs = []
        blocks = [read(g) for g in range(4)]
        for p in range(4):
            out = None
            for g in range(4):
                shift = ((g - p) * CAPC) % LANE
                turned = pltpu.roll(blocks[g], shift, 1) if shift else blocks[g]
                out = turned if out is None else jnp.where(lane_group == g, turned, out)
            outs.append(out)
        return outs

    def copies(combo):
        return [
            pltpu.make_async_remote_copy(
                src_ref=sbuf.at[combo, p],
                dst_ref=rbuf.at[combo, p],
                send_sem=send_sem.at[combo, p],
                recv_sem=recv_sem.at[combo, p],
                device_id=(targets[p],),
                device_id_type=pl.DeviceIdType.MESH,
            )
            for p in range(PEERS)
        ]

    def send_cluster(c, combo):
        def put(q, pick):
            ghost_stage[q * FR : (q + 1) * FR, :] = pick

        ghost_stage = fl.at[0 : 4 * PACK, 0:LANE]
        ghost_stage[ROWS : 4 * PACK, :] = jnp.zeros((4 * PACK - ROWS, LANE), F32)
        gather_traces(combo, onehot_send[c], meta_send[c], LANE, put)
        outs = transpose_blocks(lambda g: ghost_stage[g * PACK : (g + 1) * PACK, :])
        for p in range(PEERS):
            sbuf[combo, p] = outs[p]
        for copy in copies(combo):
            copy.start()

    def gather_tile(tile, table):
        def put(q, pick):
            seen[tile, q * FR : (q + 1) * FR, :] = pick

        gather_traces(table, onehot[tile], meta[tile, 0], 4 * LANE, put)

    def receive_cluster(c, combo):
        for copy in copies(combo):
            copy.wait()
        outs = transpose_blocks(lambda p: rbuf[combo, p])
        full = jnp.concatenate(outs, axis=0)
        hi, lo = hi_lo(full)
        ghost[c, :, 0:LANE] = hi
        ghost[c, :, LANE : 2 * LANE] = lo

    def correct_tile(tile, c):
        base = pl.multiple_of(tile * LANE, LANE)
        lanes = pl.ds(base, LANE)
        gath[0 : 4 * PACK, :] = jnp.dot(
            ghost[c], onehot_ghost[tile], preferred_element_type=F32
        )
        code = meta[tile, 1]
        is_one, is_two = [jnp.concatenate([code == i] * 3, axis=0) for i in (1, 2)]
        zero = jnp.zeros((8, 4 * LANE), F32)
        for q in range(NQ):
            cut = slice(q * FR, (q + 1) * FR)
            arrived = seen[tile, cut, :] + gath[cut, :]
            hi, lo = hi_lo(jnp.concatenate([arrived, zero], axis=0))
            x = jnp.concatenate([hi, lo, hi], axis=0)
            t = jnp.dot(m_orient[:, 0:96], x, preferred_element_type=F32)
            seen[tile, cut, :] = jnp.where(
                is_two, t[2 * FR : 3 * FR], jnp.where(is_one, t[FR : 2 * FR], t[0:FR])
            )
        half_top = 0.5 * top_out[n_levels]
        lam, mu2, mu, irho = [-0.5 * coef[tile, 21 + i] for i in range(4)]
        for f in range(4):
            normal = [[coef[tile, 9 + 3 * f + j] for j in range(3)]]
            for r in range(3):
                inner = [
                    own[tile, f * FR + r * 8 : f * FR + r * 8 + 8, q * LANE : (q + 1) * LANE]
                    for q in range(NQ)
                ]
                outer = [
                    seen[
                        tile, q * FR + r * 8 : q * FR + r * 8 + 8, f * LANE : (f + 1) * LANE
                    ]
                    for q in range(NQ)
                ]
                both = [a + b for a, b in zip(inner, outer)]
                vals = star(normal, lam, mu2, mu, irho, lambda xi, q: both[q])
                for q in range(NQ):
                    row = f * FR + r * 8
                    fl[row : row + 8, q * LANE : (q + 1) * LANE] = vals[q] + half_top * (
                        inner[q] - outer[q]
                    )
        for i in range(6):
            for q in range(NQ):
                col = q * LANE
                store_split(
                    x_lift, i * 16, col, 96, fl[i * 16 : i * 16 + 16, col : col + LANE], LANE
                )
        der[0:64, :] = jnp.dot(m_lift[:, 0:288], x_lift[...], preferred_element_type=F32)
        for q in range(NQ):
            out_ref[q, :, lanes] = out_ref[q, :, lanes] - der[0:NB, q * LANE : (q + 1) * LANE]


    acc[...] = jnp.zeros_like(acc)
    w_tick = [time_weights(i, i + 1) for i in range(4)]

    def tables_2(v, ticks):
        j0, j1, j2, j3 = ticks
        first, second = j0 + j1, j2 + j3
        whole = first + second
        return [(0, j0), (1, j1), (2, j2), (3, j3), (4, first), (5, second), (6, whole)], whole

    def predict_2(i, carry):
        predict(3 + i, tables_2, w_tick)
        return carry

    if n_levels > 2:
        top_finish(1)
        top_start(2)
    lax.fori_loop(0, 4, predict_2, 0)
    if n_levels > 3:
        top_finish(2)
        top_start(3)

    def tick(t, carry):
        half = t // 2
        odd = t - 2 * half
        last = t // 3

        @pl.when(odd == 0)
        def _():
            def tables_1(v, ticks):
                j0, j1 = ticks
                pair = j0 + j1
                return [(t, j0), (t + 1, j1), (4 + half, pair)], pair

            def tables_1_all(i):
                def inner(v, ticks):
                    entries, pair = tables_1(v, ticks)
                    whole = pair + acc[2 + i, v * 8 : v * 8 + 8, :]
                    acc[2 + i, v * 8 : v * 8 + 8, :] = whole
                    return entries + [(6, whole)], pair

                return inner

            def predict_1(i, carry):
                predict(1 + i, tables_1_all(i), w_tick[:2])
                return carry

            lax.fori_loop(0, 2, predict_1, 0)

        keep = (1 - odd).astype(F32)

        def tables_0(v, ticks):
            (j0,) = ticks
            rows_v = slice(v * 8, v * 8 + 8)
            pair = j0 + acc[0, rows_v, :]
            acc[0, rows_v, :] = pair * keep
            whole = j0 + acc[1, rows_v, :]
            acc[1, rows_v, :] = whole
            return [(t, j0), (4 + half, pair), (6, whole)], j0

        predict(0, tables_0, w_tick[:1])

        n_due = 1 + odd + last
        n_tiles = 1 + 2 * odd + 4 * last

        def combo_of(a, b):
            return (1 - a) * t + (a - b) * (4 + half) + b * 6

        def send_step(c, carry):
            a = (c + 1) // 2
            b = c // 2
            send_cluster(c, combo_of(a, b))
            return carry

        def gather_step(j, carry):
            a = (j + 6) // 7
            b = (j + 4) // 7
            gather_tile(j, combo_of(a, b))
            return carry

        def receive_step(c, carry):
            a = (c + 1) // 2
            b = c // 2
            receive_cluster(c, combo_of(a, b))
            return carry

        def correct_step(j, carry):
            correct_tile(j, (j + 6) // 7 + (j + 4) // 7)
            return carry

        lax.fori_loop(0, n_due, send_step, 0)
        lax.fori_loop(0, n_tiles, gather_step, 0)
        @pl.when(t == 0)
        def _():
            top_finish(n_levels - 1)

        lax.fori_loop(0, n_due, receive_step, 0)
        lax.fori_loop(0, n_tiles, correct_step, 0)
        return carry

    lax.fori_loop(0, 4, tick, 0)


def local(
    dof_state,
    jacobian_inv,
    face_normals,
    material,
    deriv_mats,
    stiff_mats,
    trace_mats,
    lift_mats,
    orient_mats,
    nbr_slot,
    nbr_face,
    orient_code,
    send_list,
):
    n_dev = lax.axis_size("dom")
    radices = []
    while math.prod(radices) < n_dev:
        radices.append(min(4, n_dev // math.prod(radices)))
    vmem = pl.BlockSpec(memory_space=pltpu.VMEM)

    def run(*refs):
        kernel(n_dev, radices, *refs)

    return pl.pallas_call(
        run,
        out_shape=jax.ShapeDtypeStruct((NQ, NB, ELEMS), F32),
        in_specs=[vmem] * 13,
        out_specs=vmem,
        scratch_shapes=[
            *[pltpu.VMEM((m, LANE * -(-3 * k // LANE)), BF16) for m, k in zip(level_m, level_k)],
            pltpu.VMEM((STIFF_M, 2 * LANE), BF16),
            pltpu.VMEM((96, 2 * LANE), BF16),
            pltpu.VMEM((80, LANE), BF16),
            pltpu.VMEM((64, 3 * LANE), BF16),
            pltpu.VMEM((STIFF_M, LANE), F32),
            pltpu.VMEM((3, 8, LANE), jnp.int32),
            pltpu.VMEM((len(radices) + 1, 8, LANE), F32),
            pltpu.VMEM((len(radices), 3, 8, LANE), F32),
            pltpu.SemaphoreType.DMA((len(radices), 3)),
            pltpu.SemaphoreType.DMA((len(radices), 3)),
            pltpu.VMEM((TILES, 25, 8, LANE), F32),
            pltpu.VMEM((7, 1024, ELEMS), BF16),
            pltpu.VMEM((TILES, ELEMS, 4 * LANE), BF16),
            pltpu.VMEM((3, ELEMS, LANE), BF16),
            pltpu.VMEM((TILES, 2 * LANE, 4 * LANE), BF16),
            pltpu.VMEM((TILES, 2, 8, 4 * LANE), jnp.int32),
            pltpu.VMEM((3, 8, LANE), jnp.int32),
            pltpu.VMEM((TILES, 96, NQ * LANE), F32),
            pltpu.VMEM((TILES, ROWS, 4 * LANE), F32),
            pltpu.VMEM((1024, 4 * LANE), F32),
            pltpu.VMEM((STIFF_M, NQ * LANE), F32),
            pltpu.VMEM((192, NQ * LANE), BF16),
            pltpu.VMEM((NQ, 40, LANE), F32),
            pltpu.VMEM((NQ, 24, LANE), F32),
            pltpu.VMEM((NQ, 16, LANE), F32),
            pltpu.VMEM((NQ, 8, LANE), F32),
            pltpu.VMEM((NQ, 8, LANE), F32),
            pltpu.VMEM((4, NQ * NB, LANE), F32),
            pltpu.VMEM((4 * PACK, NQ * LANE), F32),
            pltpu.VMEM((288, NQ * LANE), BF16),
            pltpu.VMEM((3, 4 * PACK, 2 * LANE), BF16),
            pltpu.VMEM((7, PEERS, PACK, LANE), F32),
            pltpu.VMEM((7, PEERS, PACK, LANE), F32),
            pltpu.SemaphoreType.DMA((7, PEERS)),
            pltpu.SemaphoreType.DMA((7, PEERS)),
        ],
        compiler_params=pltpu.CompilerParams(
            collective_id=0, has_side_effects=True, vmem_limit_bytes=58 * 1024 * 1024
        ),
        cost_estimate=pl.CostEstimate(
            flops=25_000_000_000, bytes_accessed=6_000_000, transcendentals=0
        ),
    )(
        dof_state,
        jacobian_inv,
        jnp.transpose(face_normals, (1, 0, 2)),
        material,
        deriv_mats,
        stiff_mats,
        jnp.transpose(trace_mats, (1, 0, 2)),
        jnp.transpose(lift_mats, (2, 0, 1)),
        orient_mats,
        nbr_slot,
        nbr_face,
        orient_code,
        jnp.transpose(send_list, (1, 0, 2)),
    )


def solution(mesh):
    return jax.shard_map(
        local,
        mesh=mesh,
        in_specs=(
            P(None, None, "dom"),
            P(None, None, "dom"),
            P(None, None, "dom"),
            P(None, "dom"),
            P(),
            P(),
            P(),
            P(),
            P(),
            P(None, "dom"),
            P(None, "dom"),
            P(None, "dom"),
            P(None, None, "dom"),
        ),
        out_specs=P(None, None, "dom"),
        check_vma=False,
    )
```

```python
import math

import jax
import jax.numpy as jnp
from jax import lax
from jax.experimental import pallas as pl
from jax.experimental.pallas import tpu as pltpu
from jax.sharding import PartitionSpec as P

NQ = 9
NB = 56
NF = 21
FR = 24
LANE = 128
TILES = 7
PEERS = 4
CAPC = 32
ELEMS = TILES * LANE
F32 = jnp.float32
BF16 = jnp.bfloat16

step_size = 0.04
peer_offsets = (-2, -1, 1, 2)
level_rows = (56, 40, 24, 16, 8, 8)
level_k = (64, 48, 32, 16, 16)
level_m = (128, 80, 48, 32, 32)
sizes = (56, 35, 20, 10, 4, 1)
STIFF_M = 272
ROWS = NQ * FR
PACK = 56
SLOTS = 3


def time_weights(lower, upper):
    return [
        step_size ** (k + 1) * (upper ** (k + 1) - lower ** (k + 1)) / math.factorial(k + 1)
        for k in range(6)
    ]


def hi_lo(x):
    hi = x.astype(BF16)
    return hi, (x - hi.astype(F32)).astype(BF16)


def kernel(
    n_dev,
    radices,
    state_in,
    jac_ref,
    nrm_ref,
    mat_ref,
    deriv_ref,
    stiff_ref,
    trace_ref,
    lift_ref,
    orient_ref,
    slot_ref,
    face_ref,
    code_ref,
    send_ref,
    out_ref,
    m0,
    m1,
    m2,
    m3,
    m4,
    m_stiff,
    m_trace,
    m_orient,
    m_lift,
    stage,
    send_stage,
    top_out,
    top_in,
    top_send_sem,
    top_recv_sem,
    coef,
    tabs,
    onehot,
    onehot_send,
    onehot_ghost,
    meta,
    meta_send,
    own,
    seen,
    gath_all,
    der_all,
    x3_all,
    lv1,
    lv2,
    lv3,
    lv4,
    lv5,
    acc,
    integrals,
    fl_all,
    x_lift_all,
    ghost,
    sbuf,
    rbuf,
    send_sem,
    recv_sem,
):
    me = lax.axis_index("dom")
    targets = [lax.rem(me + n_dev + off, n_dev) for off in peer_offsets]
    level_mats = (m0, m1, m2, m3, m4)
    levels_all = (lv1, lv2, lv3, lv4, lv5)
    partners = []
    stride = 1
    for radix in radices:
        place = lax.rem(me // stride, radix)
        partners.append(
            [me + (lax.rem(place + i, radix) - place) * stride for i in range(1, radix)]
        )
        stride *= radix
    greeted = targets + [dev for group in partners for dev in group]
    barrier = pltpu.get_barrier_semaphore()
    for dev in greeted:
        pl.semaphore_signal(barrier, inc=1, device_id=(dev,), device_id_type=pl.DeviceIdType.MESH)

    mat = mat_ref[...]
    inv_rho = 1.0 / mat[0:1]
    speed = jnp.sqrt((mat[1:2] + 2.0 * mat[2:3]) * inv_rho)
    top_out[0] = jnp.broadcast_to(jnp.max(speed, axis=1, keepdims=True), (8, LANE))

    def top_copies(level):
        return [
            pltpu.make_async_remote_copy(
                src_ref=top_out.at[level],
                dst_ref=top_in.at[level, i],
                send_sem=top_send_sem.at[level, i],
                recv_sem=top_recv_sem.at[level, i],
                device_id=(dev,),
                device_id_type=pl.DeviceIdType.MESH,
            )
            for i, dev in enumerate(partners[level])
        ]

    def top_start(level):
        for copy in top_copies(level):
            copy.start()

    def top_finish(level):
        for copy in top_copies(level):
            copy.wait()
        best = top_out[level]
        for i in range(len(partners[level])):
            best = jnp.maximum(best, top_in[level, i])
        top_out[level + 1] = best

    n_levels = len(radices)
    lane_of = lax.broadcasted_iota(jnp.int32, (stage.shape[0], LANE), 1)

    def lay(m_ref, rows, k_pad, base):
        hi = base.astype(BF16).astype(F32)
        lo = base - hi
        cols = [None] * (m_ref.shape[1] // LANE)
        for i, part in enumerate((hi, hi, lo)):
            at = i * k_pad
            col, off = divmod(at, LANE)
            turned = pltpu.roll(part, off, 1) if off else part
            if off + k_pad <= LANE:
                pieces = [(col, turned)]
            else:
                wide = lane_of[0:rows] >= off
                pieces = [(col, jnp.where(wide, turned, 0.0)), (col + 1, jnp.where(wide, 0.0, turned))]
            for c, piece in pieces:
                cols[c] = piece if cols[c] is None else cols[c] + piece
        for c, piece in enumerate(cols):
            m_ref[:, c * LANE : (c + 1) * LANE] = piece.astype(BF16)

    def clear():
        stage[...] = jnp.zeros_like(stage)

    for k, m_ref in enumerate(level_mats):
        n_in, n_out = sizes[k], sizes[k + 1]
        clear()
        for xi in range(3):
            row = xi * level_rows[k + 1]
            stage[row : row + n_out, 0:n_in] = deriv_ref[xi, 0:n_out, 0:n_in]
        lay(m_ref, level_m[k], level_k[k], stage[0 : level_m[k], :])
    clear()
    for xi in range(3):
        stage[xi * NB : (xi + 1) * NB, 0:NB] = stiff_ref[xi]
    for f in range(4):
        row = 3 * NB + f * FR
        stage[row : row + NF, 0:NB] = trace_ref[:, f, :]
    lay(m_stiff, STIFF_M, 64, stage[0:STIFF_M, :])
    lay(m_trace, 96, 64, stage[3 * NB : 3 * NB + 96, :])
    clear()
    for h in range(3):
        stage[h * FR : h * FR + NF, 0:NF] = orient_ref[h]
    lay(m_orient, 80, 32, stage[0:80, :])
    clear()
    for f in range(4):
        stage[f * FR : f * FR + NF, 0:NB] = lift_ref[:, f, :]
    lay(m_lift, 64, 96, jnp.transpose(stage[0:LANE, :])[0:64, :])

    out_ref[...] = state_in[...]
    pl.semaphore_wait(barrier, len(greeted))
    top_start(0)
    rows = [jac_ref[xi][j : j + 1] for xi in range(3) for j in range(3)]
    rows += [nrm_ref[j][f : f + 1] for f in range(4) for j in range(3)]
    rows += [mat[1:2], 2.0 * mat[2:3], mat[2:3], inv_rho]
    for t in range(TILES):
        for i, row in enumerate(rows):
            coef[t, i] = jnp.broadcast_to(row[:, t * LANE : (t + 1) * LANE], (8, LANE))

    slots = slot_ref[...]
    faces = face_ref[...]
    codes = code_ref[...]
    away = slots - ELEMS
    peer = (
        (away >= 96).astype(jnp.int32)
        + (away >= 192).astype(jnp.int32)
        + (away >= 288).astype(jnp.int32)
    )
    ghost_col = jnp.where(away >= 0, peer * CAPC + (away & (CAPC - 1)), -1)
    elem_rows = lax.broadcasted_iota(jnp.int32, (ELEMS, LANE), 0)
    ghost_rows = lax.broadcasted_iota(jnp.int32, (LANE, LANE), 0)

    def hot(rows_iota, line):
        return jnp.where(rows_iota == line, 1.0, 0.0).astype(BF16)

    for t in range(TILES):
        for f in range(4):
            cut = slice(t * LANE, (t + 1) * LANE)
            at = slice(f * LANE, (f + 1) * LANE)
            onehot[t, :, at] = hot(elem_rows, slots[f : f + 1, cut])
            g = hot(ghost_rows, ghost_col[f : f + 1, cut])
            onehot_ghost[t, 0:LANE, at] = g
            onehot_ghost[t, LANE : 2 * LANE, at] = g
            meta[t, 0, :, at] = jnp.broadcast_to(faces[f : f + 1, cut], (8, LANE))
            meta[t, 1, :, at] = jnp.broadcast_to(codes[f : f + 1, cut], (8, LANE))
    send_stage[...] = jnp.zeros_like(send_stage)
    send_lane = lax.broadcasted_iota(jnp.int32, (1, LANE), 1) // CAPC
    for c in range(3):
        send_stage[c, 0:PEERS, 0:CAPC] = send_ref[c]
    lines = []
    for c in range(3):
        line = send_stage[c, 0:1, :]
        for p in range(1, PEERS):
            turned = pltpu.roll(send_stage[c], p * CAPC, 1)[p : p + 1]
            line = jnp.where(send_lane == p, turned, line)
        lines.append(line)
    for c in range(3):
        onehot_send[c] = hot(elem_rows, jnp.where(lines[c] >= 0, lines[c] >> 2, -1))
        meta_send[c] = jnp.broadcast_to(lines[c] & 3, (8, LANE))


    def star_rows(c, read):
        n_xi = len(c)

        def total(pairs):
            out = None
            for xi in range(n_xi):
                for j, q in pairs:
                    term = c[xi][j] * vals[xi][q]
                    out = term if out is None else out + term
            return out

        vals = [[read(xi, q) for q in range(NQ)] for xi in range(n_xi)]
        return total

    def star(c, lam, mu2, mu, irho, read):
        total = star_rows(c, read)
        p = total([(0, 6)])
        q = total([(1, 7)])
        r = total([(2, 8)])
        div = lam * (p + q + r)
        return [
            div + mu2 * p,
            div + mu2 * q,
            div + mu2 * r,
            mu * total([(1, 6), (0, 7)]),
            mu * total([(2, 7), (1, 8)]),
            mu * total([(2, 6), (0, 8)]),
            irho * total([(0, 0), (1, 3), (2, 5)]),
            irho * total([(0, 3), (1, 1), (2, 4)]),
            irho * total([(0, 5), (1, 4), (2, 2)]),
        ]

    def store_split(ref, row, col, k_pad, x, width):
        hi, lo = hi_lo(x)
        ref[row : row + 16, col : col + width] = hi
        ref[k_pad + row : k_pad + row + 16, col : col + width] = lo
        ref[2 * k_pad + row : 2 * k_pad + row + 16, col : col + width] = hi

    def put_operand(ref, k_pad, q, pieces):
        if len(pieces) % 2:
            pieces = pieces + [jnp.zeros((8, LANE), F32)]
        for i in range(0, len(pieces), 2):
            pair = jnp.concatenate([pieces[i], pieces[i + 1]], axis=0)
            store_split(ref, i * 8, q * LANE, k_pad, pair, LANE)

    def predict(tile, slot, table_of, weights, keep_integral=None):
        base = pl.multiple_of(tile * LANE, LANE)
        lanes = pl.ds(base, LANE)
        cj = [[coef[tile, 3 * xi + j] for j in range(3)] for xi in range(3)]
        lam, mu2, mu, irho = [coef[tile, 21 + i] for i in range(4)]
        x3, der = x3_all.at[slot], der_all.at[slot]
        level_refs = [None] + [lv.at[slot] for lv in levels_all]
        for q in range(NQ):
            put_operand(x3, 64, q, [out_ref[q, r * 8 : r * 8 + 8, lanes] for r in range(7)])
        yield
        for k in range(5):
            kp = level_k[k]
            m = level_m[k]
            der[0:m, :] = jnp.dot(
                level_mats[k][:, 0 : 3 * kp], x3[0 : 3 * kp, :], preferred_element_type=F32
            )
            yield
            n = level_rows[k + 1]
            pend = [[] for _ in range(NQ)]
            for r in range(n // 8):

                def read(xi, q, r=r):
                    lo_row = xi * n + r * 8
                    return der[lo_row : lo_row + 8, q * LANE : (q + 1) * LANE]

                vals = star(cj, lam, mu2, mu, irho, read)
                for q in range(NQ):
                    level_refs[k + 1][q, r * 8 : r * 8 + 8, :] = vals[q]
                    pend[q].append(vals[q])
                last = r == n // 8 - 1
                if k < 4 and (r % 2 == 1 or last):
                    for q in range(NQ):
                        lo_piece = pend[q][0]
                        hi_piece = pend[q][1] if len(pend[q]) == 2 else jnp.zeros((8, LANE), F32)
                        pair = jnp.concatenate([lo_piece, hi_piece], axis=0)
                        store_split(x3, (r // 2) * 16, q * LANE, level_k[k + 1], pair, LANE)
                if r % 2 == 1 or last:
                    pend = [[] for _ in range(NQ)]
            yield
        own_pend = [[] for _ in range(NQ)]
        held = {}
        for v in range(64):
            if v < 63:
                q, r = divmod(v, 7)
                terms = [out_ref[q, r * 8 : r * 8 + 8, lanes]]
                for k in range(1, 6):
                    if r * 8 < level_rows[k]:
                        terms.append(level_refs[k][q, r * 8 : r * 8 + 8, :])
                ticks = []
                for w in weights:
                    total = terms[0] * w[0]
                    for k in range(1, len(terms)):
                        total = total + terms[k] * w[k]
                    ticks.append(total)
                entries, own_int = table_of(v, ticks)
                if keep_integral is not None:
                    keep_integral[v * 8 : v * 8 + 8, :] = own_int
                else:
                    own_pend[q].append(own_int)
                    if r == 6:
                        put_operand(x3, 64, q, own_pend[q])
            else:
                entries = [(idx, jnp.zeros((8, LANE), F32)) for idx, _ in entries]
            if v % 2 == 0:
                held = entries
            else:
                for (idx, first), (_, second) in zip(held, entries):
                    hi, lo = hi_lo(jnp.concatenate([first, second], axis=0))
                    row = (v // 2) * 16
                    tabs[idx, row : row + 16, lanes] = hi
                    tabs[idx, 512 + row : 512 + row + 16, lanes] = lo
        yield
        if keep_integral is None:
            yield from volume(tile, slot, None)

    def volume(tile, slot, integral):
        base = pl.multiple_of(tile * LANE, LANE)
        lanes = pl.ds(base, LANE)
        cj = [[coef[tile, 3 * xi + j] for j in range(3)] for xi in range(3)]
        lam, mu2, mu, irho = [coef[tile, 21 + i] for i in range(4)]
        x3, der = x3_all.at[slot], der_all.at[slot]
        if integral is not None:
            for q in range(NQ):
                put_operand(
                    x3, 64, q, [integral[(q * 7 + r) * 8 : (q * 7 + r) * 8 + 8, :] for r in range(7)]
                )
            yield
        der[...] = jnp.dot(m_stiff[:, 0:192], x3[...], preferred_element_type=F32)
        yield
        for r in range(7):

            def read(xi, q, r=r):
                lo_row = xi * NB + r * 8
                return der[lo_row : lo_row + 8, q * LANE : (q + 1) * LANE]

            vals = star(cj, lam, mu2, mu, irho, read)
            for q in range(NQ):
                out_ref[q, r * 8 : r * 8 + 8, lanes] = (
                    out_ref[q, r * 8 : r * 8 + 8, lanes] - vals[q]
                )
        own[tile] = der[168 : 168 + 96, :]
        yield

    def gather_traces(slot, table, hot_mat, face_rows, width, put):
        gath = gath_all.at[slot]
        gath[:, 0:width] = jnp.dot(tabs[table], hot_mat, preferred_element_type=F32)
        yield
        is_one, is_two, is_three = [
            jnp.concatenate([face_rows == i] * 3, axis=0) for i in (1, 2, 3)
        ]
        zero = jnp.zeros((8, width), F32)
        for q in range(NQ):
            hi = jnp.concatenate([gath[q * NB : (q + 1) * NB, 0:width], zero], axis=0).astype(BF16)
            lo = jnp.concatenate(
                [gath[512 + q * NB : 512 + (q + 1) * NB, 0:width], zero], axis=0
            ).astype(BF16)
            x = jnp.concatenate([hi, lo, hi], axis=0)
            t = jnp.dot(m_trace[:, 0:192], x, preferred_element_type=F32)
            pick = jnp.where(
                is_three,
                t[3 * FR : 4 * FR],
                jnp.where(
                    is_two, t[2 * FR : 3 * FR], jnp.where(is_one, t[FR : 2 * FR], t[0:FR])
                ),
            )
            put(q, pick)
            yield

    def together(*tasks):
        tasks = list(tasks)
        while tasks:
            for task in list(tasks):
                if next(task, "end") == "end":
                    tasks.remove(task)

    lane_group = lax.broadcasted_iota(jnp.int32, (PACK, LANE), 1) // CAPC

    def transpose_blocks(read):
        outs = []
        blocks = [read(g) for g in range(4)]
        for p in range(4):
            out = None
            for g in range(4):
                shift = ((g - p) * CAPC) % LANE
                turned = pltpu.roll(blocks[g], shift, 1) if shift else blocks[g]
                out = turned if out is None else jnp.where(lane_group == g, turned, out)
            outs.append(out)
        return outs

    def copies(combo):
        return [
            pltpu.make_async_remote_copy(
                src_ref=sbuf.at[combo, p],
                dst_ref=rbuf.at[combo, p],
                send_sem=send_sem.at[combo, p],
                recv_sem=recv_sem.at[combo, p],
                device_id=(targets[p],),
                device_id_type=pl.DeviceIdType.MESH,
            )
            for p in range(PEERS)
        ]

    def send_cluster(c, combo, slot):
        staged = fl_all.at[slot, 0 : 4 * PACK, 0:LANE]

        def put(q, pick):
            staged[q * FR : (q + 1) * FR, :] = pick

        staged[ROWS : 4 * PACK, :] = jnp.zeros((4 * PACK - ROWS, LANE), F32)
        yield from gather_traces(slot, combo, onehot_send[c], meta_send[c], LANE, put)
        outs = transpose_blocks(lambda g: staged[g * PACK : (g + 1) * PACK, :])
        for p in range(PEERS):
            sbuf[combo, p] = outs[p]
        for copy in copies(combo):
            copy.start()
        yield

    def gather_tile(tile, table, slot):
        def put(q, pick):
            seen[tile, q * FR : (q + 1) * FR, :] = pick

        yield from gather_traces(slot, table, onehot[tile], meta[tile, 0], 4 * LANE, put)

    def receive_cluster(c, combo):
        for copy in copies(combo):
            copy.wait()
        outs = transpose_blocks(lambda p: rbuf[combo, p])
        full = jnp.concatenate(outs, axis=0)
        hi, lo = hi_lo(full)
        ghost[c, :, 0:LANE] = hi
        ghost[c, :, LANE : 2 * LANE] = lo

    def correct_tile(tile, c, slot):
        base = pl.multiple_of(tile * LANE, LANE)
        lanes = pl.ds(base, LANE)
        gath, fl, x_lift, der = gath_all.at[slot], fl_all.at[slot], x_lift_all.at[slot], der_all.at[slot]
        gath[0 : 4 * PACK, :] = jnp.dot(
            ghost[c], onehot_ghost[tile], preferred_element_type=F32
        )
        yield
        code = meta[tile, 1]
        is_one, is_two = [jnp.concatenate([code == i] * 3, axis=0) for i in (1, 2)]
        zero = jnp.zeros((8, 4 * LANE), F32)
        for q in range(NQ):
            cut = slice(q * FR, (q + 1) * FR)
            arrived = seen[tile, cut, :] + gath[cut, :]
            hi, lo = hi_lo(jnp.concatenate([arrived, zero], axis=0))
            x = jnp.concatenate([hi, lo, hi], axis=0)
            t = jnp.dot(m_orient[:, 0:96], x, preferred_element_type=F32)
            gath[512 + q * FR : 512 + (q + 1) * FR, :] = jnp.where(
                is_two, t[2 * FR : 3 * FR], jnp.where(is_one, t[FR : 2 * FR], t[0:FR])
            )
            yield
        half_top = 0.5 * top_out[n_levels]
        lam, mu2, mu, irho = [-0.5 * coef[tile, 21 + i] for i in range(4)]
        for f in range(4):
            normal = [[coef[tile, 9 + 3 * f + j] for j in range(3)]]
            for r in range(3):
                inner = [
                    own[tile, f * FR + r * 8 : f * FR + r * 8 + 8, q * LANE : (q + 1) * LANE]
                    for q in range(NQ)
                ]
                outer = [
                    gath[
                        512 + q * FR + r * 8 : 512 + q * FR + r * 8 + 8,
                        f * LANE : (f + 1) * LANE,
                    ]
                    for q in range(NQ)
                ]
                both = [a + b for a, b in zip(inner, outer)]
                vals = star(normal, lam, mu2, mu, irho, lambda xi, q: both[q])
                for q in range(NQ):
                    row = f * FR + r * 8
                    fl[row : row + 8, q * LANE : (q + 1) * LANE] = vals[q] + half_top * (
                        inner[q] - outer[q]
                    )
            if f % 2:
                for i in range(3 * (f // 2), 3 * (f // 2) + 3):
                    for q in range(NQ):
                        col = q * LANE
                        store_split(
                            x_lift, i * 16, col, 96, fl[i * 16 : i * 16 + 16, col : col + LANE], LANE
                        )
            yield
        der[0:64, :] = jnp.dot(m_lift[:, 0:288], x_lift[...], preferred_element_type=F32)
        yield
        for q in range(NQ):
            out_ref[q, :, lanes] = out_ref[q, :, lanes] - der[0:NB, q * LANE : (q + 1) * LANE]
        yield


    acc[...] = jnp.zeros_like(acc)
    w_tick = [time_weights(i, i + 1) for i in range(4)]

    def tables_2(v, ticks):
        j0, j1, j2, j3 = ticks
        first, second = j0 + j1, j2 + j3
        whole = first + second
        return [(0, j0), (1, j1), (2, j2), (3, j3), (4, first), (5, second), (6, whole)], whole

    def predict_2(i, carry):
        predict(3 + i, tables_2, w_tick)
        return carry

    def advance(level):
        if level < n_levels:
            top_finish(level)
            if level + 1 < n_levels:
                top_start(level + 1)

    def predict_2(i, carry):
        @pl.when(i == 1)
        def _():
            advance(0)

        together(
            *[
                predict(3 + 2 * i + n, n, tables_2, w_tick, integrals.at[2 * i + n])
                for n in range(2)
            ]
        )
        return carry

    lax.fori_loop(0, 2, predict_2, 0)
    advance(1)

    def two_ticks(half, carry):
        even = 2 * half
        odd = even + 1

        def tables_1(n):
            def inner(v, ticks):
                j0, j1 = ticks
                pair = j0 + j1
                rows_v = slice(v * 8, v * 8 + 8)
                whole = pair + acc[2 + n, rows_v, :]
                acc[2 + n, rows_v, :] = whole
                return [(even, j0), (odd, j1), (4 + half, pair), (6, whole)], pair

            return inner

        def tables_0_even(v, ticks):
            (j0,) = ticks
            acc[0, v * 8 : v * 8 + 8, :] = j0
            return [(even, j0)], j0

        def tables_0_odd(v, ticks):
            (j0,) = ticks
            rows_v = slice(v * 8, v * 8 + 8)
            pair = j0 + acc[0, rows_v, :]
            whole = pair + acc[1, rows_v, :]
            acc[1, rows_v, :] = whole
            return [(odd, j0), (4 + half, pair), (6, whole)], j0

        together(
            predict(0, 0, tables_0_even, w_tick[:1]),
            predict(1, 1, tables_1(0), w_tick[:2]),
            predict(2, 2, tables_1(1), w_tick[:2]),
        )

        @pl.when(half == 0)
        def _():
            advance(2)

        together(send_cluster(0, even, 0))
        together(
            gather_tile(0, even, 1),
            volume(3 + 2 * half, 0, integrals.at[2 * half]),
            volume(4 + 2 * half, 2, integrals.at[2 * half + 1]),
        )

        @pl.when(half == 0)
        def _():
            advance(3)

        receive_cluster(0, even)
        together(correct_tile(0, 0, 0))

        together(predict(0, 0, tables_0_odd, w_tick[:1]))
        together(send_cluster(0, odd, 0), send_cluster(1, 4 + half, 1))

        @pl.when(half == 1)
        def _():
            together(send_cluster(2, 6, 2))

        together(gather_tile(0, odd, 0), gather_tile(1, 4 + half, 1), gather_tile(2, 4 + half, 2))

        def gather_2(i, carry):
            together(*[gather_tile(3 + 2 * i + n, 6, n) for n in range(2)])
            return carry

        @pl.when(half == 1)
        def _():
            lax.fori_loop(0, 2, gather_2, 0)

        receive_cluster(0, odd)
        receive_cluster(1, 4 + half)
        together(correct_tile(0, 0, 0), correct_tile(1, 1, 1), correct_tile(2, 1, 2))

        def correct_2(i, carry):
            together(*[correct_tile(3 + 2 * i + n, 2, n) for n in range(2)])
            return carry

        @pl.when(half == 1)
        def _():
            receive_cluster(2, 6)
            lax.fori_loop(0, 2, correct_2, 0)

        return carry

    lax.fori_loop(0, 2, two_ticks, 0)


def local(
    dof_state,
    jacobian_inv,
    face_normals,
    material,
    deriv_mats,
    stiff_mats,
    trace_mats,
    lift_mats,
    orient_mats,
    nbr_slot,
    nbr_face,
    orient_code,
    send_list,
):
    n_dev = lax.axis_size("dom")
    radices = []
    while math.prod(radices) < n_dev:
        radices.append(min(4, n_dev // math.prod(radices)))
    vmem = pl.BlockSpec(memory_space=pltpu.VMEM)

    def run(*refs):
        kernel(n_dev, radices, *refs)

    return pl.pallas_call(
        run,
        out_shape=jax.ShapeDtypeStruct((NQ, NB, ELEMS), F32),
        in_specs=[vmem] * 13,
        out_specs=vmem,
        scratch_shapes=[
            *[pltpu.VMEM((m, LANE * -(-3 * k // LANE)), BF16) for m, k in zip(level_m, level_k)],
            pltpu.VMEM((STIFF_M, 2 * LANE), BF16),
            pltpu.VMEM((96, 2 * LANE), BF16),
            pltpu.VMEM((80, LANE), BF16),
            pltpu.VMEM((64, 3 * LANE), BF16),
            pltpu.VMEM((STIFF_M, LANE), F32),
            pltpu.VMEM((3, 8, LANE), jnp.int32),
            pltpu.VMEM((len(radices) + 1, 8, LANE), F32),
            pltpu.VMEM((len(radices), 3, 8, LANE), F32),
            pltpu.SemaphoreType.DMA((len(radices), 3)),
            pltpu.SemaphoreType.DMA((len(radices), 3)),
            pltpu.VMEM((TILES, 25, 8, LANE), F32),
            pltpu.VMEM((7, 1024, ELEMS), BF16),
            pltpu.VMEM((TILES, ELEMS, 4 * LANE), BF16),
            pltpu.VMEM((3, ELEMS, LANE), BF16),
            pltpu.VMEM((TILES, 2 * LANE, 4 * LANE), BF16),
            pltpu.VMEM((TILES, 2, 8, 4 * LANE), jnp.int32),
            pltpu.VMEM((3, 8, LANE), jnp.int32),
            pltpu.VMEM((TILES, 96, NQ * LANE), F32),
            pltpu.VMEM((TILES, ROWS, 4 * LANE), F32),
            pltpu.VMEM((SLOTS, 1024, 4 * LANE), F32),
            pltpu.VMEM((SLOTS, STIFF_M, NQ * LANE), F32),
            pltpu.VMEM((SLOTS, 192, NQ * LANE), BF16),
            pltpu.VMEM((SLOTS, NQ, 40, LANE), F32),
            pltpu.VMEM((SLOTS, NQ, 24, LANE), F32),
            pltpu.VMEM((SLOTS, NQ, 16, LANE), F32),
            pltpu.VMEM((SLOTS, NQ, 8, LANE), F32),
            pltpu.VMEM((SLOTS, NQ, 8, LANE), F32),
            pltpu.VMEM((4, NQ * NB, LANE), F32),
            pltpu.VMEM((4, NQ * NB, LANE), F32),
            pltpu.VMEM((SLOTS, 4 * PACK, NQ * LANE), F32),
            pltpu.VMEM((SLOTS, 288, NQ * LANE), BF16),
            pltpu.VMEM((3, 4 * PACK, 2 * LANE), BF16),
            pltpu.VMEM((7, PEERS, PACK, LANE), F32),
            pltpu.VMEM((7, PEERS, PACK, LANE), F32),
            pltpu.SemaphoreType.DMA((7, PEERS)),
            pltpu.SemaphoreType.DMA((7, PEERS)),
        ],
        compiler_params=pltpu.CompilerParams(
            collective_id=0, has_side_effects=True, vmem_limit_bytes=58 * 1024 * 1024
        ),
        cost_estimate=pl.CostEstimate(
            flops=25_000_000_000, bytes_accessed=6_000_000, transcendentals=0
        ),
    )(
        dof_state,
        jacobian_inv,
        jnp.transpose(face_normals, (1, 0, 2)),
        material,
        deriv_mats,
        stiff_mats,
        jnp.transpose(trace_mats, (1, 0, 2)),
        jnp.transpose(lift_mats, (2, 0, 1)),
        orient_mats,
        nbr_slot,
        nbr_face,
        orient_code,
        jnp.transpose(send_list, (1, 0, 2)),
    )


def solution(mesh):
    return jax.shard_map(
        local,
        mesh=mesh,
        in_specs=(
            P(None, None, "dom"),
            P(None, None, "dom"),
            P(None, None, "dom"),
            P(None, "dom"),
            P(),
            P(),
            P(),
            P(),
            P(),
            P(None, "dom"),
            P(None, "dom"),
            P(None, "dom"),
            P(None, None, "dom"),
        ),
        out_specs=P(None, None, "dom"),
        check_vma=False,
    )
```

```python
import math

import jax
import jax.numpy as jnp
from jax import lax
from jax.experimental import pallas as pl
from jax.experimental.pallas import tpu as pltpu
from jax.sharding import PartitionSpec as P

NQ = 9
NB = 56
NF = 21
FR = 24
LANE = 128
TILES = 7
PEERS = 4
CAPC = 32
ELEMS = TILES * LANE
F32 = jnp.float32
BF16 = jnp.bfloat16

step_size = 0.04
peer_offsets = (-2, -1, 1, 2)
level_rows = (56, 40, 24, 16, 8, 8)
level_k = (64, 48, 32, 16, 16)
level_m = (128, 80, 48, 32, 32)
sizes = (56, 35, 20, 10, 4, 1)
STIFF_M = 272
ROWS = NQ * FR
PACK = 56
SLOTS = 3


def time_weights(lower, upper):
    return [
        step_size ** (k + 1) * (upper ** (k + 1) - lower ** (k + 1)) / math.factorial(k + 1)
        for k in range(6)
    ]


def hi_lo(x):
    hi = x.astype(BF16)
    return hi, (x - hi.astype(F32)).astype(BF16)


def kernel(
    n_dev,
    radices,
    state_in,
    jac_ref,
    nrm_ref,
    mat_ref,
    deriv_ref,
    stiff_ref,
    trace_ref,
    lift_ref,
    orient_ref,
    slot_ref,
    face_ref,
    code_ref,
    send_ref,
    out_ref,
    m0,
    m1,
    m2,
    m3,
    m4,
    m_stiff,
    m_trace,
    m_orient,
    m_lift,
    stage,
    send_stage,
    top_out,
    top_in,
    top_send_sem,
    top_recv_sem,
    state_sem,
    coef,
    tabs,
    onehot,
    onehot_send,
    onehot_ghost,
    meta,
    meta_send,
    own,
    seen,
    gath_all,
    der_all,
    x3_all,
    lv1,
    lv2,
    lv3,
    lv4,
    lv5,
    acc,
    integrals,
    fl_all,
    x_lift_all,
    ghost,
    sbuf,
    rbuf,
    send_sem,
    recv_sem,
):
    me = lax.axis_index("dom")
    targets = [lax.rem(me + n_dev + off, n_dev) for off in peer_offsets]
    level_mats = (m0, m1, m2, m3, m4)
    levels_all = (lv1, lv2, lv3, lv4, lv5)
    partners = []
    stride = 1
    for radix in radices:
        place = lax.rem(me // stride, radix)
        partners.append(
            [me + (lax.rem(place + i, radix) - place) * stride for i in range(1, radix)]
        )
        stride *= radix
    greeted = targets + [dev for group in partners for dev in group]
    barrier = pltpu.get_barrier_semaphore()
    for dev in greeted:
        pl.semaphore_signal(barrier, inc=1, device_id=(dev,), device_id_type=pl.DeviceIdType.MESH)

    state_copy = pltpu.make_async_copy(state_in, out_ref, state_sem)
    state_copy.start()
    mat = mat_ref[...]
    inv_rho = 1.0 / mat[0:1]
    speed = jnp.sqrt((mat[1:2] + 2.0 * mat[2:3]) * inv_rho)
    top_out[0] = jnp.broadcast_to(jnp.max(speed, axis=1, keepdims=True), (8, LANE))

    def top_copies(level):
        return [
            pltpu.make_async_remote_copy(
                src_ref=top_out.at[level],
                dst_ref=top_in.at[level, i],
                send_sem=top_send_sem.at[level, i],
                recv_sem=top_recv_sem.at[level, i],
                device_id=(dev,),
                device_id_type=pl.DeviceIdType.MESH,
            )
            for i, dev in enumerate(partners[level])
        ]

    def top_start(level):
        for copy in top_copies(level):
            copy.start()

    def top_finish(level):
        for copy in top_copies(level):
            copy.wait()
        best = top_out[level]
        for i in range(len(partners[level])):
            best = jnp.maximum(best, top_in[level, i])
        top_out[level + 1] = best

    n_levels = len(radices)
    lane_of = lax.broadcasted_iota(jnp.int32, (stage.shape[0], LANE), 1)

    def lay(m_ref, rows, k_pad, base):
        hi = base.astype(BF16).astype(F32)
        lo = base - hi
        cols = [None] * (m_ref.shape[1] // LANE)
        for i, part in enumerate((hi, hi, lo)):
            at = i * k_pad
            col, off = divmod(at, LANE)
            turned = pltpu.roll(part, off, 1) if off else part
            if off + k_pad <= LANE:
                pieces = [(col, turned)]
            else:
                wide = lane_of[0:rows] >= off
                pieces = [(col, jnp.where(wide, turned, 0.0)), (col + 1, jnp.where(wide, 0.0, turned))]
            for c, piece in pieces:
                cols[c] = piece if cols[c] is None else cols[c] + piece
        for c, piece in enumerate(cols):
            m_ref[:, c * LANE : (c + 1) * LANE] = piece.astype(BF16)

    def clear():
        stage[...] = jnp.zeros_like(stage)

    for k, m_ref in enumerate(level_mats):
        n_in, n_out = sizes[k], sizes[k + 1]
        clear()
        for xi in range(3):
            row = xi * level_rows[k + 1]
            stage[row : row + n_out, 0:n_in] = deriv_ref[xi, 0:n_out, 0:n_in]
        lay(m_ref, level_m[k], level_k[k], stage[0 : level_m[k], :])
    clear()
    for xi in range(3):
        stage[xi * NB : (xi + 1) * NB, 0:NB] = stiff_ref[xi]
    for f in range(4):
        row = 3 * NB + f * FR
        stage[row : row + NF, 0:NB] = trace_ref[:, f, :]
    lay(m_stiff, STIFF_M, 64, stage[0:STIFF_M, :])
    lay(m_trace, 96, 64, stage[3 * NB : 3 * NB + 96, :])
    clear()
    for h in range(3):
        stage[h * FR : h * FR + NF, 0:NF] = orient_ref[h]
    lay(m_orient, 80, 32, stage[0:80, :])
    clear()
    for f in range(4):
        stage[f * FR : f * FR + NF, 0:NB] = lift_ref[:, f, :]
    lay(m_lift, 64, 96, jnp.transpose(stage[0:LANE, :])[0:64, :])

    state_copy.wait()
    rows = [jac_ref[xi][j : j + 1] for xi in range(3) for j in range(3)]
    rows += [nrm_ref[j][f : f + 1] for f in range(4) for j in range(3)]
    rows += [mat[1:2], 2.0 * mat[2:3], mat[2:3], inv_rho]
    for t in range(TILES):
        for i, row in enumerate(rows):
            coef[t, i] = jnp.broadcast_to(row[:, t * LANE : (t + 1) * LANE], (8, LANE))

    slots = slot_ref[...]
    faces = face_ref[...]
    codes = code_ref[...]
    away = slots - ELEMS
    peer = (
        (away >= 96).astype(jnp.int32)
        + (away >= 192).astype(jnp.int32)
        + (away >= 288).astype(jnp.int32)
    )
    ghost_col = jnp.where(away >= 0, peer * CAPC + (away & (CAPC - 1)), -1)
    elem_rows = lax.broadcasted_iota(jnp.int32, (ELEMS, LANE), 0)
    ghost_rows = lax.broadcasted_iota(jnp.int32, (LANE, LANE), 0)

    def hot(rows_iota, line):
        return jnp.where(rows_iota == line, 1.0, 0.0).astype(BF16)

    def build_onehots(tiles):
        for t in tiles:
            for f in range(4):
                cut = slice(t * LANE, (t + 1) * LANE)
                at = slice(f * LANE, (f + 1) * LANE)
                onehot[t, :, at] = hot(elem_rows, slots[f : f + 1, cut])
                g = hot(ghost_rows, ghost_col[f : f + 1, cut])
                onehot_ghost[t, 0:LANE, at] = g
                onehot_ghost[t, LANE : 2 * LANE, at] = g
                meta[t, 0, :, at] = jnp.broadcast_to(faces[f : f + 1, cut], (8, LANE))
                meta[t, 1, :, at] = jnp.broadcast_to(codes[f : f + 1, cut], (8, LANE))

    build_onehots([0])
    send_stage[...] = jnp.zeros_like(send_stage)
    send_lane = lax.broadcasted_iota(jnp.int32, (1, LANE), 1) // CAPC
    for c in range(3):
        send_stage[c, 0:PEERS, 0:CAPC] = send_ref[c]
    lines = []
    for c in range(3):
        line = send_stage[c, 0:1, :]
        for p in range(1, PEERS):
            turned = pltpu.roll(send_stage[c], p * CAPC, 1)[p : p + 1]
            line = jnp.where(send_lane == p, turned, line)
        lines.append(line)
    for c in range(3):
        onehot_send[c] = hot(elem_rows, jnp.where(lines[c] >= 0, lines[c] >> 2, -1))
        meta_send[c] = jnp.broadcast_to(lines[c] & 3, (8, LANE))


    def star_rows(c, read):
        n_xi = len(c)

        def total(pairs):
            out = None
            for xi in range(n_xi):
                for j, q in pairs:
                    term = c[xi][j] * vals[xi][q]
                    out = term if out is None else out + term
            return out

        vals = [[read(xi, q) for q in range(NQ)] for xi in range(n_xi)]
        return total

    def star(c, lam, mu2, mu, irho, read):
        total = star_rows(c, read)
        p = total([(0, 6)])
        q = total([(1, 7)])
        r = total([(2, 8)])
        div = lam * (p + q + r)
        return [
            div + mu2 * p,
            div + mu2 * q,
            div + mu2 * r,
            mu * total([(1, 6), (0, 7)]),
            mu * total([(2, 7), (1, 8)]),
            mu * total([(2, 6), (0, 8)]),
            irho * total([(0, 0), (1, 3), (2, 5)]),
            irho * total([(0, 3), (1, 1), (2, 4)]),
            irho * total([(0, 5), (1, 4), (2, 2)]),
        ]

    def store_split(ref, row, col, k_pad, x, width):
        hi, lo = hi_lo(x)
        ref[row : row + 16, col : col + width] = hi
        ref[k_pad + row : k_pad + row + 16, col : col + width] = lo
        ref[2 * k_pad + row : 2 * k_pad + row + 16, col : col + width] = hi

    def put_operand(ref, k_pad, q, pieces):
        if len(pieces) % 2:
            pieces = pieces + [jnp.zeros((8, LANE), F32)]
        for i in range(0, len(pieces), 2):
            pair = jnp.concatenate([pieces[i], pieces[i + 1]], axis=0)
            store_split(ref, i * 8, q * LANE, k_pad, pair, LANE)

    def predict(tile, slot, table_of, weights, keep_integral=None):
        base = pl.multiple_of(tile * LANE, LANE)
        lanes = pl.ds(base, LANE)
        cj = [[coef[tile, 3 * xi + j] for j in range(3)] for xi in range(3)]
        lam, mu2, mu, irho = [coef[tile, 21 + i] for i in range(4)]
        x3, der = x3_all.at[slot], der_all.at[slot]
        level_refs = [None] + [lv.at[slot] for lv in levels_all]
        for q in range(NQ):
            put_operand(x3, 64, q, [out_ref[q, r * 8 : r * 8 + 8, lanes] for r in range(7)])
        yield
        for k in range(5):
            kp = level_k[k]
            m = level_m[k]
            der[0:m, :] = jnp.dot(
                level_mats[k][:, 0 : 3 * kp], x3[0 : 3 * kp, :], preferred_element_type=F32
            )
            yield
            n = level_rows[k + 1]
            pend = [[] for _ in range(NQ)]
            for r in range(n // 8):

                def read(xi, q, r=r):
                    lo_row = xi * n + r * 8
                    return der[lo_row : lo_row + 8, q * LANE : (q + 1) * LANE]

                vals = star(cj, lam, mu2, mu, irho, read)
                for q in range(NQ):
                    level_refs[k + 1][q, r * 8 : r * 8 + 8, :] = vals[q]
                    pend[q].append(vals[q])
                last = r == n // 8 - 1
                if k < 4 and (r % 2 == 1 or last):
                    for q in range(NQ):
                        lo_piece = pend[q][0]
                        hi_piece = pend[q][1] if len(pend[q]) == 2 else jnp.zeros((8, LANE), F32)
                        pair = jnp.concatenate([lo_piece, hi_piece], axis=0)
                        store_split(x3, (r // 2) * 16, q * LANE, level_k[k + 1], pair, LANE)
                if r % 2 == 1 or last:
                    pend = [[] for _ in range(NQ)]
            yield
        own_pend = [[] for _ in range(NQ)]
        held = {}
        for v in range(64):
            if v < 63:
                q, r = divmod(v, 7)
                terms = [out_ref[q, r * 8 : r * 8 + 8, lanes]]
                for k in range(1, 6):
                    if r * 8 < level_rows[k]:
                        terms.append(level_refs[k][q, r * 8 : r * 8 + 8, :])
                ticks = []
                for w in weights:
                    total = terms[0] * w[0]
                    for k in range(1, len(terms)):
                        total = total + terms[k] * w[k]
                    ticks.append(total)
                entries, own_int = table_of(v, ticks)
                if keep_integral is not None:
                    keep_integral[v * 8 : v * 8 + 8, :] = own_int
                else:
                    own_pend[q].append(own_int)
                    if r == 6:
                        put_operand(x3, 64, q, own_pend[q])
            else:
                entries = [(idx, jnp.zeros((8, LANE), F32)) for idx, _ in entries]
            if v % 2 == 0:
                held = entries
            else:
                for (idx, first), (_, second) in zip(held, entries):
                    hi, lo = hi_lo(jnp.concatenate([first, second], axis=0))
                    row = (v // 2) * 16
                    tabs[idx, row : row + 16, lanes] = hi
                    tabs[idx, 512 + row : 512 + row + 16, lanes] = lo
        yield
        if keep_integral is None:
            yield from volume(tile, slot, None)

    def volume(tile, slot, integral):
        base = pl.multiple_of(tile * LANE, LANE)
        lanes = pl.ds(base, LANE)
        cj = [[coef[tile, 3 * xi + j] for j in range(3)] for xi in range(3)]
        lam, mu2, mu, irho = [coef[tile, 21 + i] for i in range(4)]
        x3, der = x3_all.at[slot], der_all.at[slot]
        if integral is not None:
            for q in range(NQ):
                put_operand(
                    x3, 64, q, [integral[(q * 7 + r) * 8 : (q * 7 + r) * 8 + 8, :] for r in range(7)]
                )
            yield
        der[...] = jnp.dot(m_stiff[:, 0:192], x3[...], preferred_element_type=F32)
        yield
        for r in range(7):

            def read(xi, q, r=r):
                lo_row = xi * NB + r * 8
                return der[lo_row : lo_row + 8, q * LANE : (q + 1) * LANE]

            vals = star(cj, lam, mu2, mu, irho, read)
            for q in range(NQ):
                out_ref[q, r * 8 : r * 8 + 8, lanes] = (
                    out_ref[q, r * 8 : r * 8 + 8, lanes] - vals[q]
                )
        own[tile] = der[168 : 168 + 96, :]
        yield

    def gather_traces(slot, table, hot_mat, face_rows, width, put):
        gath = gath_all.at[slot]
        gath[:, 0:width] = jnp.dot(tabs[table], hot_mat, preferred_element_type=F32)
        yield
        is_one, is_two, is_three = [
            jnp.concatenate([face_rows == i] * 3, axis=0) for i in (1, 2, 3)
        ]
        zero = jnp.zeros((8, width), F32)
        for q in range(NQ):
            hi = jnp.concatenate([gath[q * NB : (q + 1) * NB, 0:width], zero], axis=0).astype(BF16)
            lo = jnp.concatenate(
                [gath[512 + q * NB : 512 + (q + 1) * NB, 0:width], zero], axis=0
            ).astype(BF16)
            x = jnp.concatenate([hi, lo, hi], axis=0)
            t = jnp.dot(m_trace[:, 0:192], x, preferred_element_type=F32)
            pick = jnp.where(
                is_three,
                t[3 * FR : 4 * FR],
                jnp.where(
                    is_two, t[2 * FR : 3 * FR], jnp.where(is_one, t[FR : 2 * FR], t[0:FR])
                ),
            )
            put(q, pick)
            yield

    def together(*tasks):
        tasks = list(tasks)
        while tasks:
            for task in list(tasks):
                if next(task, "end") == "end":
                    tasks.remove(task)

    lane_group = lax.broadcasted_iota(jnp.int32, (PACK, LANE), 1) // CAPC

    def transpose_blocks(read):
        outs = []
        blocks = [read(g) for g in range(4)]
        for p in range(4):
            out = None
            for g in range(4):
                shift = ((g - p) * CAPC) % LANE
                turned = pltpu.roll(blocks[g], shift, 1) if shift else blocks[g]
                out = turned if out is None else jnp.where(lane_group == g, turned, out)
            outs.append(out)
        return outs

    def copies(combo):
        return [
            pltpu.make_async_remote_copy(
                src_ref=sbuf.at[combo, p],
                dst_ref=rbuf.at[combo, p],
                send_sem=send_sem.at[combo, p],
                recv_sem=recv_sem.at[combo, p],
                device_id=(targets[p],),
                device_id_type=pl.DeviceIdType.MESH,
            )
            for p in range(PEERS)
        ]

    def send_cluster(c, combo, slot):
        staged = fl_all.at[slot, 0 : 4 * PACK, 0:LANE]

        staged[ROWS : 4 * PACK, :] = jnp.zeros((4 * PACK - ROWS, LANE), F32)
        gath, x3, der = gath_all.at[slot], x3_all.at[slot], der_all.at[slot]
        gath[:, 0:LANE] = jnp.dot(tabs[combo], onehot_send[c], preferred_element_type=F32)
        yield
        zero = jnp.zeros((8, LANE), F32)
        for q in range(NQ):
            hi, lo = [
                jnp.concatenate([gath[row : row + NB, 0:LANE], zero], axis=0).astype(BF16)
                for row in (q * NB, 512 + q * NB)
            ]
            for i, part in enumerate((hi, lo, hi)):
                x3[64 * i : 64 * i + 64, q * LANE : (q + 1) * LANE] = part
        der[0:96, :] = jnp.dot(m_trace[:, 0:192], x3[...], preferred_element_type=F32)
        yield
        picks = [jnp.concatenate([meta_send[c] == i] * 3, axis=0) for i in (1, 2, 3)]
        for q in range(NQ):
            best = der[0:FR, q * LANE : (q + 1) * LANE]
            for i, pick in enumerate(picks):
                row = (i + 1) * FR
                best = jnp.where(pick, der[row : row + FR, q * LANE : (q + 1) * LANE], best)
            staged[q * FR : (q + 1) * FR, :] = best
        outs = transpose_blocks(lambda g: staged[g * PACK : (g + 1) * PACK, :])
        for p in range(PEERS):
            sbuf[combo, p] = outs[p]
        for copy in copies(combo):
            copy.start()
        yield

    def gather_tile(tile, table, slot):
        def put(q, pick):
            seen[tile, q * FR : (q + 1) * FR, :] = pick

        yield from gather_traces(slot, table, onehot[tile], meta[tile, 0], 4 * LANE, put)

    def receive_cluster(c, combo):
        for copy in copies(combo):
            copy.wait()
        outs = transpose_blocks(lambda p: rbuf[combo, p])
        full = jnp.concatenate(outs, axis=0)
        hi, lo = hi_lo(full)
        ghost[c, :, 0:LANE] = hi
        ghost[c, :, LANE : 2 * LANE] = lo

    def correct_tile(tile, c, slot):
        base = pl.multiple_of(tile * LANE, LANE)
        lanes = pl.ds(base, LANE)
        gath, fl, x_lift, der = gath_all.at[slot], fl_all.at[slot], x_lift_all.at[slot], der_all.at[slot]
        gath[0 : 4 * PACK, :] = jnp.dot(
            ghost[c], onehot_ghost[tile], preferred_element_type=F32
        )
        yield
        code = meta[tile, 1]
        is_one, is_two = [jnp.concatenate([code == i] * 3, axis=0) for i in (1, 2)]
        zero = jnp.zeros((8, 4 * LANE), F32)
        for q in range(NQ):
            cut = slice(q * FR, (q + 1) * FR)
            arrived = seen[tile, cut, :] + gath[cut, :]
            hi, lo = hi_lo(jnp.concatenate([arrived, zero], axis=0))
            x = jnp.concatenate([hi, lo, hi], axis=0)
            t = jnp.dot(m_orient[:, 0:96], x, preferred_element_type=F32)
            gath[512 + q * FR : 512 + (q + 1) * FR, :] = jnp.where(
                is_two, t[2 * FR : 3 * FR], jnp.where(is_one, t[FR : 2 * FR], t[0:FR])
            )
            yield
        half_top = 0.5 * top_out[n_levels]
        lam, mu2, mu, irho = [-0.5 * coef[tile, 21 + i] for i in range(4)]
        for f in range(4):
            normal = [[coef[tile, 9 + 3 * f + j] for j in range(3)]]
            for r in range(3):
                inner = [
                    own[tile, f * FR + r * 8 : f * FR + r * 8 + 8, q * LANE : (q + 1) * LANE]
                    for q in range(NQ)
                ]
                outer = [
                    gath[
                        512 + q * FR + r * 8 : 512 + q * FR + r * 8 + 8,
                        f * LANE : (f + 1) * LANE,
                    ]
                    for q in range(NQ)
                ]
                both = [a + b for a, b in zip(inner, outer)]
                vals = star(normal, lam, mu2, mu, irho, lambda xi, q: both[q])
                for q in range(NQ):
                    row = f * FR + r * 8
                    fl[row : row + 8, q * LANE : (q + 1) * LANE] = vals[q] + half_top * (
                        inner[q] - outer[q]
                    )
            if f % 2:
                for i in range(3 * (f // 2), 3 * (f // 2) + 3):
                    for q in range(NQ):
                        col = q * LANE
                        store_split(
                            x_lift, i * 16, col, 96, fl[i * 16 : i * 16 + 16, col : col + LANE], LANE
                        )
            yield
        der[0:64, :] = jnp.dot(m_lift[:, 0:288], x_lift[...], preferred_element_type=F32)
        yield
        for q in range(NQ):
            out_ref[q, :, lanes] = out_ref[q, :, lanes] - der[0:NB, q * LANE : (q + 1) * LANE]
        yield


    acc[...] = jnp.zeros_like(acc)
    w_tick = [time_weights(i, i + 1) for i in range(4)]

    def tables_2(v, ticks):
        j0, j1, j2, j3 = ticks
        first, second = j0 + j1, j2 + j3
        whole = first + second
        return [(0, j0), (1, j1), (2, j2), (3, j3), (4, first), (5, second), (6, whole)], whole

    def advance(level):
        if level < n_levels:
            top_finish(level)
            if level + 1 < n_levels:
                top_start(level + 1)

    def predict_2(first):
        together(
            *[predict(3 + n, n - first, tables_2, w_tick, integrals.at[n]) for n in (first, first + 1)]
        )

    predict_2(0)
    pl.semaphore_wait(barrier, len(greeted))
    top_start(0)
    predict_2(2)
    advance(0)

    def two_ticks(half, carry):
        even = 2 * half
        odd = even + 1

        def tables_1(n):
            def inner(v, ticks):
                j0, j1 = ticks
                pair = j0 + j1
                rows_v = slice(v * 8, v * 8 + 8)
                whole = pair + acc[2 + n, rows_v, :]
                acc[2 + n, rows_v, :] = whole
                return [(even, j0), (odd, j1), (4 + half, pair), (6, whole)], pair

            return inner

        def tables_0_even(v, ticks):
            (j0,) = ticks
            acc[0, v * 8 : v * 8 + 8, :] = j0
            return [(even, j0)], j0

        def tables_0_odd(v, ticks):
            (j0,) = ticks
            rows_v = slice(v * 8, v * 8 + 8)
            pair = j0 + acc[0, rows_v, :]
            whole = pair + acc[1, rows_v, :]
            acc[1, rows_v, :] = whole
            return [(odd, j0), (4 + half, pair), (6, whole)], j0

        together(
            predict(0, 0, tables_0_even, w_tick[:1], integrals.at[4]),
            predict(1, 1, tables_1(0), w_tick[:2], integrals.at[5]),
            predict(2, 2, tables_1(1), w_tick[:2], integrals.at[6]),
        )

        @pl.when(half == 0)
        def _():
            advance(1)

        together(send_cluster(0, even, 0))

        @pl.when(half == 0)
        def _():
            advance(2)
            build_onehots(range(1, TILES))

        together(
            gather_tile(0, even, 1),
            volume(0, 0, integrals.at[4]),
            volume(1, 1, integrals.at[5]),
            volume(2, 2, integrals.at[6]),
        )
        together(
            volume(3 + 2 * half, 0, integrals.at[2 * half]),
            volume(4 + 2 * half, 1, integrals.at[2 * half + 1]),
        )

        @pl.when(half == 0)
        def _():
            advance(3)

        receive_cluster(0, even)
        together(correct_tile(0, 0, 0))

        together(predict(0, 0, tables_0_odd, w_tick[:1], integrals.at[4]))
        together(send_cluster(0, odd, 0), send_cluster(1, 4 + half, 1))

        @pl.when(half == 1)
        def _():
            together(send_cluster(2, 6, 2))

        together(
            gather_tile(0, odd, 0),
            volume(0, 0, integrals.at[4]),
            gather_tile(1, 4 + half, 1),
            gather_tile(2, 4 + half, 2),
        )

        def gather_2(i, carry):
            together(*[gather_tile(3 + 2 * i + n, 6, n) for n in range(2)])
            return carry

        @pl.when(half == 1)
        def _():
            lax.fori_loop(0, 2, gather_2, 0)

        receive_cluster(0, odd)
        receive_cluster(1, 4 + half)
        together(correct_tile(0, 0, 0), correct_tile(1, 1, 1), correct_tile(2, 1, 2))

        def correct_2(i, carry):
            together(*[correct_tile(3 + 2 * i + n, 2, n) for n in range(2)])
            return carry

        @pl.when(half == 1)
        def _():
            receive_cluster(2, 6)
            lax.fori_loop(0, 2, correct_2, 0)

        return carry

    lax.fori_loop(0, 2, two_ticks, 0)


def local(
    dof_state,
    jacobian_inv,
    face_normals,
    material,
    deriv_mats,
    stiff_mats,
    trace_mats,
    lift_mats,
    orient_mats,
    nbr_slot,
    nbr_face,
    orient_code,
    send_list,
):
    n_dev = lax.axis_size("dom")
    radices = []
    while math.prod(radices) < n_dev:
        radices.append(min(4, n_dev // math.prod(radices)))
    vmem = pl.BlockSpec(memory_space=pltpu.VMEM)

    def run(*refs):
        kernel(n_dev, radices, *refs)

    return pl.pallas_call(
        run,
        out_shape=jax.ShapeDtypeStruct((NQ, NB, ELEMS), F32),
        in_specs=[pl.BlockSpec(memory_space=pl.ANY)] + [vmem] * 12,
        out_specs=vmem,
        scratch_shapes=[
            *[pltpu.VMEM((m, LANE * -(-3 * k // LANE)), BF16) for m, k in zip(level_m, level_k)],
            pltpu.VMEM((STIFF_M, 2 * LANE), BF16),
            pltpu.VMEM((96, 2 * LANE), BF16),
            pltpu.VMEM((80, LANE), BF16),
            pltpu.VMEM((64, 3 * LANE), BF16),
            pltpu.VMEM((STIFF_M, LANE), F32),
            pltpu.VMEM((3, 8, LANE), jnp.int32),
            pltpu.VMEM((len(radices) + 1, 8, LANE), F32),
            pltpu.VMEM((len(radices), 3, 8, LANE), F32),
            pltpu.SemaphoreType.DMA((len(radices), 3)),
            pltpu.SemaphoreType.DMA((len(radices), 3)),
            pltpu.SemaphoreType.DMA,
            pltpu.VMEM((TILES, 25, 8, LANE), F32),
            pltpu.VMEM((7, 1024, ELEMS), BF16),
            pltpu.VMEM((TILES, ELEMS, 4 * LANE), BF16),
            pltpu.VMEM((3, ELEMS, LANE), BF16),
            pltpu.VMEM((TILES, 2 * LANE, 4 * LANE), BF16),
            pltpu.VMEM((TILES, 2, 8, 4 * LANE), jnp.int32),
            pltpu.VMEM((3, 8, LANE), jnp.int32),
            pltpu.VMEM((TILES, 96, NQ * LANE), F32),
            pltpu.VMEM((TILES, ROWS, 4 * LANE), F32),
            pltpu.VMEM((SLOTS, 1024, 4 * LANE), F32),
            pltpu.VMEM((SLOTS, STIFF_M, NQ * LANE), F32),
            pltpu.VMEM((SLOTS, 192, NQ * LANE), BF16),
            pltpu.VMEM((SLOTS, NQ, 40, LANE), F32),
            pltpu.VMEM((SLOTS, NQ, 24, LANE), F32),
            pltpu.VMEM((SLOTS, NQ, 16, LANE), F32),
            pltpu.VMEM((SLOTS, NQ, 8, LANE), F32),
            pltpu.VMEM((SLOTS, NQ, 8, LANE), F32),
            pltpu.VMEM((4, NQ * NB, LANE), F32),
            pltpu.VMEM((7, NQ * NB, LANE), F32),
            pltpu.VMEM((SLOTS, 4 * PACK, NQ * LANE), F32),
            pltpu.VMEM((SLOTS, 288, NQ * LANE), BF16),
            pltpu.VMEM((3, 4 * PACK, 2 * LANE), BF16),
            pltpu.VMEM((7, PEERS, PACK, LANE), F32),
            pltpu.VMEM((7, PEERS, PACK, LANE), F32),
            pltpu.SemaphoreType.DMA((7, PEERS)),
            pltpu.SemaphoreType.DMA((7, PEERS)),
        ],
        compiler_params=pltpu.CompilerParams(
            collective_id=0, has_side_effects=True, vmem_limit_bytes=58 * 1024 * 1024
        ),
        cost_estimate=pl.CostEstimate(
            flops=25_000_000_000, bytes_accessed=6_000_000, transcendentals=0
        ),
    )(
        dof_state,
        jacobian_inv,
        jnp.transpose(face_normals, (1, 0, 2)),
        material,
        deriv_mats,
        stiff_mats,
        jnp.transpose(trace_mats, (1, 0, 2)),
        jnp.transpose(lift_mats, (2, 0, 1)),
        orient_mats,
        nbr_slot,
        nbr_face,
        orient_code,
        jnp.transpose(send_list, (1, 0, 2)),
    )


def solution(mesh):
    return jax.shard_map(
        local,
        mesh=mesh,
        in_specs=(
            P(None, None, "dom"),
            P(None, None, "dom"),
            P(None, None, "dom"),
            P(None, "dom"),
            P(),
            P(),
            P(),
            P(),
            P(),
            P(None, "dom"),
            P(None, "dom"),
            P(None, "dom"),
            P(None, None, "dom"),
        ),
        out_specs=P(None, None, "dom"),
        check_vma=False,
    )
```

```python
import math

import jax
import jax.numpy as jnp
from jax import lax
from jax.experimental import pallas as pl
from jax.experimental.pallas import tpu as pltpu
from jax.sharding import PartitionSpec as P

NQ = 9
NB = 56
NF = 21
FR = 24
LANE = 128
TILES = 7
PEERS = 4
CAPC = 32
ELEMS = TILES * LANE
F32 = jnp.float32
BF16 = jnp.bfloat16

step_size = 0.04
peer_offsets = (-2, -1, 1, 2)
level_rows = (56, 40, 24, 16, 8, 8)
level_k = (64, 48, 32, 16, 16)
level_m = (128, 80, 48, 32, 32)
sizes = (56, 35, 20, 10, 4, 1)
STIFF_M = 272
ROWS = NQ * FR
PACK = 56
SLOTS = 3


def time_weights(lower, upper):
    return [
        step_size ** (k + 1) * (upper ** (k + 1) - lower ** (k + 1)) / math.factorial(k + 1)
        for k in range(6)
    ]


def hi_lo(x):
    hi = x.astype(BF16)
    return hi, (x - hi.astype(F32)).astype(BF16)


def kernel(
    n_dev,
    radices,
    state_in,
    jac_ref,
    nrm_ref,
    mat_ref,
    deriv_ref,
    stiff_ref,
    trace_ref,
    lift_ref,
    orient_ref,
    slot_ref,
    face_ref,
    code_ref,
    send_ref,
    out_ref,
    m0,
    m1,
    m2,
    m3,
    m4,
    m_stiff,
    m_trace,
    m_orient,
    m_lift,
    stage,
    send_stage,
    top_out,
    top_in,
    top_send_sem,
    top_recv_sem,
    state_sem,
    coef,
    tabs,
    onehot,
    onehot_send,
    onehot_ghost,
    meta,
    meta_send,
    own,
    seen,
    gath_all,
    der_all,
    x3_all,
    lv1,
    lv2,
    lv3,
    lv4,
    lv5,
    acc,
    integrals,
    fl_all,
    x_lift_all,
    ghost,
    sbuf,
    rbuf,
    send_sem,
    recv_sem,
):
    me = lax.axis_index("dom")
    targets = [lax.rem(me + n_dev + off, n_dev) for off in peer_offsets]
    level_mats = (m0, m1, m2, m3, m4)
    levels_all = (lv1, lv2, lv3, lv4, lv5)
    partners = []
    stride = 1
    for radix in radices:
        place = lax.rem(me // stride, radix)
        partners.append(
            [me + (lax.rem(place + i, radix) - place) * stride for i in range(1, radix)]
        )
        stride *= radix
    greeted = targets + [dev for group in partners for dev in group]
    barrier = pltpu.get_barrier_semaphore()
    for dev in greeted:
        pl.semaphore_signal(barrier, inc=1, device_id=(dev,), device_id_type=pl.DeviceIdType.MESH)

    state_copy = pltpu.make_async_copy(state_in, out_ref, state_sem)
    state_copy.start()
    mat = mat_ref[...]
    inv_rho = 1.0 / mat[0:1]
    speed = jnp.sqrt((mat[1:2] + 2.0 * mat[2:3]) * inv_rho)
    top_out[0] = jnp.broadcast_to(jnp.max(speed, axis=1, keepdims=True), (8, LANE))

    def top_copies(level):
        return [
            pltpu.make_async_remote_copy(
                src_ref=top_out.at[level],
                dst_ref=top_in.at[level, i],
                send_sem=top_send_sem.at[level, i],
                recv_sem=top_recv_sem.at[level, i],
                device_id=(dev,),
                device_id_type=pl.DeviceIdType.MESH,
            )
            for i, dev in enumerate(partners[level])
        ]

    def top_start(level):
        for copy in top_copies(level):
            copy.start()

    def top_finish(level):
        for copy in top_copies(level):
            copy.wait()
        best = top_out[level]
        for i in range(len(partners[level])):
            best = jnp.maximum(best, top_in[level, i])
        top_out[level + 1] = best

    n_levels = len(radices)
    lane_of = lax.broadcasted_iota(jnp.int32, (stage.shape[0], LANE), 1)

    def lay(m_ref, rows, k_pad, base):
        hi = base.astype(BF16).astype(F32)
        lo = base - hi
        cols = [None] * (m_ref.shape[1] // LANE)
        for i, part in enumerate((hi, hi, lo)):
            at = i * k_pad
            col, off = divmod(at, LANE)
            turned = pltpu.roll(part, off, 1) if off else part
            if off + k_pad <= LANE:
                pieces = [(col, turned)]
            else:
                wide = lane_of[0:rows] >= off
                pieces = [(col, jnp.where(wide, turned, 0.0)), (col + 1, jnp.where(wide, 0.0, turned))]
            for c, piece in pieces:
                cols[c] = piece if cols[c] is None else cols[c] + piece
        for c, piece in enumerate(cols):
            m_ref[:, c * LANE : (c + 1) * LANE] = piece.astype(BF16)

    def clear():
        stage[...] = jnp.zeros_like(stage)

    for k, m_ref in enumerate(level_mats):
        n_in, n_out = sizes[k], sizes[k + 1]
        clear()
        for xi in range(3):
            row = xi * level_rows[k + 1]
            stage[row : row + n_out, 0:n_in] = deriv_ref[xi, 0:n_out, 0:n_in]
        lay(m_ref, level_m[k], level_k[k], stage[0 : level_m[k], :])
    clear()
    for xi in range(3):
        stage[xi * NB : (xi + 1) * NB, 0:NB] = stiff_ref[xi]
    for f in range(4):
        row = 3 * NB + f * FR
        stage[row : row + NF, 0:NB] = trace_ref[:, f, :]
    lay(m_stiff, STIFF_M, 64, stage[0:STIFF_M, :])
    lay(m_trace, 96, 64, stage[3 * NB : 3 * NB + 96, :])
    clear()
    for h in range(3):
        stage[h * FR : h * FR + NF, 0:NF] = orient_ref[h]
    lay(m_orient, 80, 32, stage[0:80, :])
    clear()
    for f in range(4):
        stage[f * FR : f * FR + NF, 0:NB] = lift_ref[:, f, :]
    lay(m_lift, 64, 96, jnp.transpose(stage[0:LANE, :])[0:64, :])

    state_copy.wait()
    rows = [jac_ref[xi][j : j + 1] for xi in range(3) for j in range(3)]
    rows += [nrm_ref[j][f : f + 1] for f in range(4) for j in range(3)]
    rows += [mat[1:2], 2.0 * mat[2:3], mat[2:3], inv_rho]
    for t in range(TILES):
        for i, row in enumerate(rows):
            coef[t, i] = jnp.broadcast_to(row[:, t * LANE : (t + 1) * LANE], (8, LANE))

    slots = slot_ref[...]
    faces = face_ref[...]
    codes = code_ref[...]
    away = slots - ELEMS
    peer = (
        (away >= 96).astype(jnp.int32)
        + (away >= 192).astype(jnp.int32)
        + (away >= 288).astype(jnp.int32)
    )
    ghost_col = jnp.where(away >= 0, peer * CAPC + (away & (CAPC - 1)), -1)
    elem_rows = lax.broadcasted_iota(jnp.int32, (ELEMS, LANE), 0)
    ghost_rows = lax.broadcasted_iota(jnp.int32, (LANE, LANE), 0)

    def hot(rows_iota, line):
        return jnp.where(rows_iota == line, 1.0, 0.0).astype(BF16)

    def build_onehots(tiles):
        for t in tiles:
            for f in range(4):
                cut = slice(t * LANE, (t + 1) * LANE)
                at = slice(f * LANE, (f + 1) * LANE)
                onehot[t, :, at] = hot(elem_rows, slots[f : f + 1, cut])
                g = hot(ghost_rows, ghost_col[f : f + 1, cut])
                onehot_ghost[t, 0:LANE, at] = g
                onehot_ghost[t, LANE : 2 * LANE, at] = g
                meta[t, 0, :, at] = jnp.broadcast_to(faces[f : f + 1, cut], (8, LANE))
                meta[t, 1, :, at] = jnp.broadcast_to(codes[f : f + 1, cut], (8, LANE))

    build_onehots([0])
    send_stage[...] = jnp.zeros_like(send_stage)
    send_lane = lax.broadcasted_iota(jnp.int32, (1, LANE), 1) // CAPC
    for c in range(3):
        send_stage[c, 0:PEERS, 0:CAPC] = send_ref[c]
    lines = []
    for c in range(3):
        line = send_stage[c, 0:1, :]
        for p in range(1, PEERS):
            turned = pltpu.roll(send_stage[c], p * CAPC, 1)[p : p + 1]
            line = jnp.where(send_lane == p, turned, line)
        lines.append(line)
    for c in range(3):
        onehot_send[c] = hot(elem_rows, jnp.where(lines[c] >= 0, lines[c] >> 2, -1))
        meta_send[c] = jnp.broadcast_to(lines[c] & 3, (8, LANE))


    def star_rows(c, read):
        n_xi = len(c)

        def total(pairs):
            out = None
            for xi in range(n_xi):
                for j, q in pairs:
                    term = c[xi][j] * vals[xi][q]
                    out = term if out is None else out + term
            return out

        vals = [[read(xi, q) for q in range(NQ)] for xi in range(n_xi)]
        return total

    def star(c, lam, mu2, mu, irho, read):
        total = star_rows(c, read)
        p = total([(0, 6)])
        q = total([(1, 7)])
        r = total([(2, 8)])
        div = lam * (p + q + r)
        return [
            div + mu2 * p,
            div + mu2 * q,
            div + mu2 * r,
            mu * total([(1, 6), (0, 7)]),
            mu * total([(2, 7), (1, 8)]),
            mu * total([(2, 6), (0, 8)]),
            irho * total([(0, 0), (1, 3), (2, 5)]),
            irho * total([(0, 3), (1, 1), (2, 4)]),
            irho * total([(0, 5), (1, 4), (2, 2)]),
        ]

    def store_split(ref, row, col, k_pad, x, width):
        hi, lo = hi_lo(x)
        ref[row : row + 16, col : col + width] = hi
        ref[k_pad + row : k_pad + row + 16, col : col + width] = lo
        ref[2 * k_pad + row : 2 * k_pad + row + 16, col : col + width] = hi

    def put_operand(ref, k_pad, q, pieces):
        if len(pieces) % 2:
            pieces = pieces + [jnp.zeros((8, LANE), F32)]
        for i in range(0, len(pieces), 2):
            pair = jnp.concatenate([pieces[i], pieces[i + 1]], axis=0)
            store_split(ref, i * 8, q * LANE, k_pad, pair, LANE)

    def predict(tile, slot, table_of, weights, keep_integral=None):
        base = pl.multiple_of(tile * LANE, LANE)
        lanes = pl.ds(base, LANE)
        cj = [[coef[tile, 3 * xi + j] for j in range(3)] for xi in range(3)]
        lam, mu2, mu, irho = [coef[tile, 21 + i] for i in range(4)]
        x3, der = x3_all.at[slot], der_all.at[slot]
        level_refs = [None] + [lv.at[slot] for lv in levels_all]
        for q in range(NQ):
            put_operand(x3, 64, q, [out_ref[q, r * 8 : r * 8 + 8, lanes] for r in range(7)])
        yield
        for k in range(5):
            kp = level_k[k]
            m = level_m[k]
            der[0:m, :] = jnp.dot(
                level_mats[k][:, 0 : 3 * kp], x3[0 : 3 * kp, :], preferred_element_type=F32
            )
            yield
            n = level_rows[k + 1]
            pend = [[] for _ in range(NQ)]
            for r in range(n // 8):

                def read(xi, q, r=r):
                    lo_row = xi * n + r * 8
                    return der[lo_row : lo_row + 8, q * LANE : (q + 1) * LANE]

                vals = star(cj, lam, mu2, mu, irho, read)
                for q in range(NQ):
                    level_refs[k + 1][q, r * 8 : r * 8 + 8, :] = vals[q]
                    pend[q].append(vals[q])
                last = r == n // 8 - 1
                if k < 4 and (r % 2 == 1 or last):
                    for q in range(NQ):
                        lo_piece = pend[q][0]
                        hi_piece = pend[q][1] if len(pend[q]) == 2 else jnp.zeros((8, LANE), F32)
                        pair = jnp.concatenate([lo_piece, hi_piece], axis=0)
                        store_split(x3, (r // 2) * 16, q * LANE, level_k[k + 1], pair, LANE)
                if r % 2 == 1 or last:
                    pend = [[] for _ in range(NQ)]
            yield
        own_pend = [[] for _ in range(NQ)]
        held = {}
        for v in range(64):
            if v < 63:
                q, r = divmod(v, 7)
                terms = [out_ref[q, r * 8 : r * 8 + 8, lanes]]
                for k in range(1, 6):
                    if r * 8 < level_rows[k]:
                        terms.append(level_refs[k][q, r * 8 : r * 8 + 8, :])
                ticks = []
                for w in weights:
                    total = terms[0] * w[0]
                    for k in range(1, len(terms)):
                        total = total + terms[k] * w[k]
                    ticks.append(total)
                entries, own_int = table_of(v, ticks)
                if keep_integral is not None:
                    keep_integral[v * 8 : v * 8 + 8, :] = own_int
                else:
                    own_pend[q].append(own_int)
                    if r == 6:
                        put_operand(x3, 64, q, own_pend[q])
            else:
                entries = [(idx, jnp.zeros((8, LANE), F32)) for idx, _ in entries]
            if v % 2 == 0:
                held = entries
            else:
                for (idx, first), (_, second) in zip(held, entries):
                    hi, lo = hi_lo(jnp.concatenate([first, second], axis=0))
                    row = (v // 2) * 16
                    tabs[idx, row : row + 16, lanes] = hi
                    tabs[idx, 512 + row : 512 + row + 16, lanes] = lo
        yield
        if keep_integral is None:
            yield from volume(tile, slot, None)

    def volume(tile, slot, integral):
        base = pl.multiple_of(tile * LANE, LANE)
        lanes = pl.ds(base, LANE)
        cj = [[coef[tile, 3 * xi + j] for j in range(3)] for xi in range(3)]
        lam, mu2, mu, irho = [coef[tile, 21 + i] for i in range(4)]
        x3, der = x3_all.at[slot], der_all.at[slot]
        if integral is not None:
            for q in range(NQ):
                put_operand(
                    x3, 64, q, [integral[(q * 7 + r) * 8 : (q * 7 + r) * 8 + 8, :] for r in range(7)]
                )
            yield
        der[...] = jnp.dot(m_stiff[:, 0:192], x3[...], preferred_element_type=F32)
        yield
        for r in range(7):

            def read(xi, q, r=r):
                lo_row = xi * NB + r * 8
                return der[lo_row : lo_row + 8, q * LANE : (q + 1) * LANE]

            vals = star(cj, lam, mu2, mu, irho, read)
            for q in range(NQ):
                out_ref[q, r * 8 : r * 8 + 8, lanes] = (
                    out_ref[q, r * 8 : r * 8 + 8, lanes] - vals[q]
                )
        own[tile] = der[168 : 168 + 96, :]
        yield

    def gather_traces(slot, table, hot_mat, face_rows, width, put):
        gath = gath_all.at[slot]
        gath[:, 0:width] = jnp.dot(tabs[table], hot_mat, preferred_element_type=F32)
        yield
        is_one, is_two, is_three = [
            jnp.concatenate([face_rows == i] * 3, axis=0) for i in (1, 2, 3)
        ]
        zero = jnp.zeros((8, width), F32)
        for q in range(NQ):
            hi = jnp.concatenate([gath[q * NB : (q + 1) * NB, 0:width], zero], axis=0).astype(BF16)
            lo = jnp.concatenate(
                [gath[512 + q * NB : 512 + (q + 1) * NB, 0:width], zero], axis=0
            ).astype(BF16)
            x = jnp.concatenate([hi, lo, hi], axis=0)
            t = jnp.dot(m_trace[:, 0:192], x, preferred_element_type=F32)
            pick = jnp.where(
                is_three,
                t[3 * FR : 4 * FR],
                jnp.where(
                    is_two, t[2 * FR : 3 * FR], jnp.where(is_one, t[FR : 2 * FR], t[0:FR])
                ),
            )
            put(q, pick)
            yield

    def together(*tasks):
        tasks = list(tasks)
        while tasks:
            for task in list(tasks):
                if next(task, "end") == "end":
                    tasks.remove(task)

    lane_group = lax.broadcasted_iota(jnp.int32, (PACK, LANE), 1) // CAPC

    def transpose_blocks(read):
        outs = []
        blocks = [read(g) for g in range(4)]
        for p in range(4):
            out = None
            for g in range(4):
                shift = ((g - p) * CAPC) % LANE
                turned = pltpu.roll(blocks[g], shift, 1) if shift else blocks[g]
                out = turned if out is None else jnp.where(lane_group == g, turned, out)
            outs.append(out)
        return outs

    def copies(combo):
        return [
            pltpu.make_async_remote_copy(
                src_ref=sbuf.at[combo, p],
                dst_ref=rbuf.at[combo, p],
                send_sem=send_sem.at[combo, p],
                recv_sem=recv_sem.at[combo, p],
                device_id=(targets[p],),
                device_id_type=pl.DeviceIdType.MESH,
            )
            for p in range(PEERS)
        ]

    def send_cluster(c, combo, slot):
        staged = fl_all.at[slot, 0 : 4 * PACK, 0:LANE]

        staged[ROWS : 4 * PACK, :] = jnp.zeros((4 * PACK - ROWS, LANE), F32)
        gath, x3, der = gath_all.at[slot], x3_all.at[slot], der_all.at[slot]
        gath[:, 0:LANE] = jnp.dot(tabs[combo], onehot_send[c], preferred_element_type=F32)
        yield
        zero = jnp.zeros((8, LANE), F32)
        for q in range(NQ):
            hi, lo = [
                jnp.concatenate([gath[row : row + NB, 0:LANE], zero], axis=0).astype(BF16)
                for row in (q * NB, 512 + q * NB)
            ]
            for i, part in enumerate((hi, lo, hi)):
                x3[64 * i : 64 * i + 64, q * LANE : (q + 1) * LANE] = part
        der[0:96, :] = jnp.dot(m_trace[:, 0:192], x3[...], preferred_element_type=F32)
        yield
        picks = [jnp.concatenate([meta_send[c] == i] * 3, axis=0) for i in (1, 2, 3)]
        for q in range(NQ):
            best = der[0:FR, q * LANE : (q + 1) * LANE]
            for i, pick in enumerate(picks):
                row = (i + 1) * FR
                best = jnp.where(pick, der[row : row + FR, q * LANE : (q + 1) * LANE], best)
            staged[q * FR : (q + 1) * FR, :] = best
        outs = transpose_blocks(lambda g: staged[g * PACK : (g + 1) * PACK, :])
        for p in range(PEERS):
            sbuf[combo, p] = outs[p]
        for copy in copies(combo):
            copy.start()
        yield

    def gather_tile(tile, table, slot):
        def put(q, pick):
            seen[tile, q * FR : (q + 1) * FR, :] = pick

        yield from gather_traces(slot, table, onehot[tile], meta[tile, 0], 4 * LANE, put)

    def receive_cluster(c, combo):
        for copy in copies(combo):
            copy.wait()
        outs = transpose_blocks(lambda p: rbuf[combo, p])
        full = jnp.concatenate(outs, axis=0)
        hi, lo = hi_lo(full)
        ghost[c, :, 0:LANE] = hi
        ghost[c, :, LANE : 2 * LANE] = lo

    def correct_tile(tile, c, slot):
        base = pl.multiple_of(tile * LANE, LANE)
        lanes = pl.ds(base, LANE)
        gath, fl, x_lift, der = gath_all.at[slot], fl_all.at[slot], x_lift_all.at[slot], der_all.at[slot]
        gath[0 : 4 * PACK, :] = jnp.dot(
            ghost[c], onehot_ghost[tile], preferred_element_type=F32
        )
        yield
        code = meta[tile, 1]
        is_one, is_two = [jnp.concatenate([code == i] * 3, axis=0) for i in (1, 2)]
        zero = jnp.zeros((8, 4 * LANE), F32)
        for q in range(NQ):
            cut = slice(q * FR, (q + 1) * FR)
            arrived = seen[tile, cut, :] + gath[cut, :]
            hi, lo = hi_lo(jnp.concatenate([arrived, zero], axis=0))
            x = jnp.concatenate([hi, lo, hi], axis=0)
            t = jnp.dot(m_orient[:, 0:96], x, preferred_element_type=F32)
            gath[512 + q * FR : 512 + (q + 1) * FR, :] = jnp.where(
                is_two, t[2 * FR : 3 * FR], jnp.where(is_one, t[FR : 2 * FR], t[0:FR])
            )
            yield
        half_top = 0.5 * top_out[n_levels]
        lam, mu2, mu, irho = [-0.5 * coef[tile, 21 + i] for i in range(4)]
        for f in range(4):
            normal = [[coef[tile, 9 + 3 * f + j] for j in range(3)]]
            for r in range(3):
                inner = [
                    own[tile, f * FR + r * 8 : f * FR + r * 8 + 8, q * LANE : (q + 1) * LANE]
                    for q in range(NQ)
                ]
                outer = [
                    gath[
                        512 + q * FR + r * 8 : 512 + q * FR + r * 8 + 8,
                        f * LANE : (f + 1) * LANE,
                    ]
                    for q in range(NQ)
                ]
                both = [a + b for a, b in zip(inner, outer)]
                vals = star(normal, lam, mu2, mu, irho, lambda xi, q: both[q])
                for q in range(NQ):
                    row = f * FR + r * 8
                    fl[row : row + 8, q * LANE : (q + 1) * LANE] = vals[q] + half_top * (
                        inner[q] - outer[q]
                    )
            if f % 2:
                for i in range(3 * (f // 2), 3 * (f // 2) + 3):
                    for q in range(NQ):
                        col = q * LANE
                        store_split(
                            x_lift, i * 16, col, 96, fl[i * 16 : i * 16 + 16, col : col + LANE], LANE
                        )
            yield
        der[0:64, :] = jnp.dot(m_lift[:, 0:288], x_lift[...], preferred_element_type=F32)
        yield
        for q in range(NQ):
            out_ref[q, :, lanes] = out_ref[q, :, lanes] - der[0:NB, q * LANE : (q + 1) * LANE]
        yield


    acc[...] = jnp.zeros_like(acc)
    w_tick = [time_weights(i, i + 1) for i in range(4)]

    def tables_2(v, ticks):
        j0, j1, j2, j3 = ticks
        first, second = j0 + j1, j2 + j3
        whole = first + second
        return [(0, j0), (1, j1), (2, j2), (3, j3), (4, first), (5, second), (6, whole)], whole

    def advance(level):
        if level < n_levels:
            top_finish(level)
            if level + 1 < n_levels:
                top_start(level + 1)

    def predict_2(first):
        together(
            *[predict(3 + n, n - first, tables_2, w_tick, integrals.at[n]) for n in (first, first + 1)]
        )

    predict_2(0)
    pl.semaphore_wait(barrier, len(greeted))
    top_start(0)
    predict_2(2)
    advance(0)

    def two_ticks(half, carry):
        even = 2 * half
        odd = even + 1

        def tables_1(n):
            def inner(v, ticks):
                j0, j1 = ticks
                pair = j0 + j1
                rows_v = slice(v * 8, v * 8 + 8)
                whole = pair + acc[2 + n, rows_v, :]
                acc[2 + n, rows_v, :] = whole
                return [(even, j0), (odd, j1), (4 + half, pair), (6, whole)], pair

            return inner

        def tables_0_even(v, ticks):
            (j0,) = ticks
            acc[0, v * 8 : v * 8 + 8, :] = j0
            return [(even, j0)], j0

        def tables_0_odd(v, ticks):
            (j0,) = ticks
            rows_v = slice(v * 8, v * 8 + 8)
            pair = j0 + acc[0, rows_v, :]
            whole = pair + acc[1, rows_v, :]
            acc[1, rows_v, :] = whole
            return [(odd, j0), (4 + half, pair), (6, whole)], j0

        together(
            predict(0, 0, tables_0_even, w_tick[:1], integrals.at[4]),
            predict(1, 1, tables_1(0), w_tick[:2], integrals.at[5]),
            predict(2, 2, tables_1(1), w_tick[:2], integrals.at[6]),
        )

        @pl.when(half == 0)
        def _():
            advance(1)

        together(send_cluster(0, even, 0))

        @pl.when(half == 0)
        def _():
            advance(2)
            build_onehots(range(1, TILES))

        together(
            gather_tile(0, even, 1),
            volume(0, 0, integrals.at[4]),
            volume(1, 1, integrals.at[5]),
            volume(2, 2, integrals.at[6]),
        )
        @pl.when(half == 1)
        def _():
            together(volume(5, 0, integrals.at[2]), volume(6, 1, integrals.at[3]))

        @pl.when(half == 0)
        def _():
            advance(3)

        receive_cluster(0, even)
        together(correct_tile(0, 0, 0))

        together(predict(0, 0, tables_0_odd, w_tick[:1], integrals.at[4]))
        together(send_cluster(0, odd, 0), send_cluster(1, 4 + half, 1))

        @pl.when(half == 1)
        def _():
            together(send_cluster(2, 6, 2))

        @pl.when(half == 0)
        def _():
            together(volume(3, 0, integrals.at[0]), volume(4, 1, integrals.at[1]))

        together(
            gather_tile(0, odd, 0),
            volume(0, 0, integrals.at[4]),
            gather_tile(1, 4 + half, 1),
            gather_tile(2, 4 + half, 2),
        )

        @pl.when(half == 1)
        def _():
            together(*[gather_tile(3 + n, 6, n) for n in range(2)])
            together(*[gather_tile(5 + n, 6, n) for n in range(2)])

        receive_cluster(0, odd)
        receive_cluster(1, 4 + half)
        together(correct_tile(0, 0, 0), correct_tile(1, 1, 1), correct_tile(2, 1, 2))

        @pl.when(half == 1)
        def _():
            receive_cluster(2, 6)
            together(*[correct_tile(3 + n, 2, n) for n in range(2)])
            together(*[correct_tile(5 + n, 2, n) for n in range(2)])

        return carry

    lax.fori_loop(0, 2, two_ticks, 0)


def local(
    dof_state,
    jacobian_inv,
    face_normals,
    material,
    deriv_mats,
    stiff_mats,
    trace_mats,
    lift_mats,
    orient_mats,
    nbr_slot,
    nbr_face,
    orient_code,
    send_list,
):
    n_dev = lax.axis_size("dom")
    radices = []
    while math.prod(radices) < n_dev:
        radices.append(min(4, n_dev // math.prod(radices)))
    vmem = pl.BlockSpec(memory_space=pltpu.VMEM)

    def run(*refs):
        kernel(n_dev, radices, *refs)

    return pl.pallas_call(
        run,
        out_shape=jax.ShapeDtypeStruct((NQ, NB, ELEMS), F32),
        in_specs=[pl.BlockSpec(memory_space=pl.ANY)] + [vmem] * 12,
        out_specs=vmem,
        scratch_shapes=[
            *[pltpu.VMEM((m, LANE * -(-3 * k // LANE)), BF16) for m, k in zip(level_m, level_k)],
            pltpu.VMEM((STIFF_M, 2 * LANE), BF16),
            pltpu.VMEM((96, 2 * LANE), BF16),
            pltpu.VMEM((80, LANE), BF16),
            pltpu.VMEM((64, 3 * LANE), BF16),
            pltpu.VMEM((STIFF_M, LANE), F32),
            pltpu.VMEM((3, 8, LANE), jnp.int32),
            pltpu.VMEM((len(radices) + 1, 8, LANE), F32),
            pltpu.VMEM((len(radices), 3, 8, LANE), F32),
            pltpu.SemaphoreType.DMA((len(radices), 3)),
            pltpu.SemaphoreType.DMA((len(radices), 3)),
            pltpu.SemaphoreType.DMA,
            pltpu.VMEM((TILES, 25, 8, LANE), F32),
            pltpu.VMEM((7, 1024, ELEMS), BF16),
            pltpu.VMEM((TILES, ELEMS, 4 * LANE), BF16),
            pltpu.VMEM((3, ELEMS, LANE), BF16),
            pltpu.VMEM((TILES, 2 * LANE, 4 * LANE), BF16),
            pltpu.VMEM((TILES, 2, 8, 4 * LANE), jnp.int32),
            pltpu.VMEM((3, 8, LANE), jnp.int32),
            pltpu.VMEM((TILES, 96, NQ * LANE), F32),
            pltpu.VMEM((TILES, ROWS, 4 * LANE), F32),
            pltpu.VMEM((SLOTS, 1024, 4 * LANE), F32),
            pltpu.VMEM((SLOTS, STIFF_M, NQ * LANE), F32),
            pltpu.VMEM((SLOTS, 192, NQ * LANE), BF16),
            pltpu.VMEM((SLOTS, NQ, 40, LANE), F32),
            pltpu.VMEM((SLOTS, NQ, 24, LANE), F32),
            pltpu.VMEM((SLOTS, NQ, 16, LANE), F32),
            pltpu.VMEM((SLOTS, NQ, 8, LANE), F32),
            pltpu.VMEM((SLOTS, NQ, 8, LANE), F32),
            pltpu.VMEM((4, NQ * NB, LANE), F32),
            pltpu.VMEM((7, NQ * NB, LANE), F32),
            pltpu.VMEM((SLOTS, 4 * PACK, NQ * LANE), F32),
            pltpu.VMEM((SLOTS, 288, NQ * LANE), BF16),
            pltpu.VMEM((3, 4 * PACK, 2 * LANE), BF16),
            pltpu.VMEM((7, PEERS, PACK, LANE), F32),
            pltpu.VMEM((7, PEERS, PACK, LANE), F32),
            pltpu.SemaphoreType.DMA((7, PEERS)),
            pltpu.SemaphoreType.DMA((7, PEERS)),
        ],
        compiler_params=pltpu.CompilerParams(
            collective_id=0, has_side_effects=True, vmem_limit_bytes=58 * 1024 * 1024
        ),
        cost_estimate=pl.CostEstimate(
            flops=25_000_000_000, bytes_accessed=6_000_000, transcendentals=0
        ),
    )(
        dof_state,
        jacobian_inv,
        jnp.transpose(face_normals, (1, 0, 2)),
        material,
        deriv_mats,
        stiff_mats,
        jnp.transpose(trace_mats, (1, 0, 2)),
        jnp.transpose(lift_mats, (2, 0, 1)),
        orient_mats,
        nbr_slot,
        nbr_face,
        orient_code,
        jnp.transpose(send_list, (1, 0, 2)),
    )


def solution(mesh):
    return jax.shard_map(
        local,
        mesh=mesh,
        in_specs=(
            P(None, None, "dom"),
            P(None, None, "dom"),
            P(None, None, "dom"),
            P(None, "dom"),
            P(),
            P(),
            P(),
            P(),
            P(),
            P(None, "dom"),
            P(None, "dom"),
            P(None, "dom"),
            P(None, None, "dom"),
        ),
        out_specs=P(None, None, "dom"),
        check_vma=False,
    )
```
